32 devices in a mesh: row: 8 (over z, x), col: 4 (over y, core).
Axes of the slice: x: 2, y: 2, z: 4, core: 2. Of those that a mesh axis runs over, the one named last changes fastest.
Arguments:
- normed: bfloat16 [64, 6144], P('row', 'col'), may hold values from -6 to 6
- out_grad: bfloat16 [64, 6144], P('row', 'col'), may hold values from -6 to 6
- up_weight: bfloat16 [6144, 24576], P('col', 'row'), may hold values from -0.078125 to 0.078125
- up_bias: bfloat16 [24576], P('row'), may hold values from -3 to 3
- down_weight: bfloat16 [24576, 6144], P('row', 'col'), may hold values from -0.0390625 to 0.0390625
Outputs:
- in_grad: bfloat16 [64, 6144], P('row', 'col')
- up_grad: float32 [6144, 24576], P('col', 'row')
- bias_grad: float32 [24576], P('row')
- down_grad: float32 [24576, 6144], P('row', 'col')
The draws below stay inside these ranges and needn't reach their ends.
All inputs are finite; a program needn't handle non-finite values.
Results may differ from the reference program's by a relative error of at most 0.0049.
Values may be sent and summed in bfloat16 or wider, within the bound.
No kernel may reach another device: no remote copies, remote signals or barrier semaphores. Data moves between devices by JAX's collectives and lax.ppermute only.
A program may use at most 128 MiB of HBM per device.

```python
import math
import jax
import jax.numpy as jnp
from jax import lax

D = 6144
FF = 24576
TOKENS = 64


def levels(own_key, shape, pieces, smallest, high):
    level = 1.0
    for axis_at, blocks in pieces:
        draws = jax.random.uniform(jax.random.fold_in(jax.random.fold_in(own_key, 6), axis_at), (blocks,), jnp.float32, smallest / len(pieces), high / len(pieces))
        level = level * jnp.repeat(jnp.exp(draws), shape[axis_at] // blocks).reshape((-1,) + (1,) * (len(shape) - 1 - axis_at))
    return level


def scatter_about(rng, dims, width, most, pieces=(), held_as=jnp.bfloat16):
    result = width * jax.random.normal(rng, dims, jnp.float32)
    if pieces:
        result = result * levels(rng, dims, pieces, -0.22, 0.18)
    return jnp.clip(result, -most, most).astype(held_as)


def setup_inputs(seed: int = 0) -> dict:
    arg_keys = jax.random.split(jax.random.key(seed), 6)
    normed = scatter_about(arg_keys[0], (TOKENS, D), 1.0, 6.0, ((0, 8), (1, 4)))
    out_grad = scatter_about(arg_keys[1], (TOKENS, D), 1.0, 6.0, ((0, 8), (1, 4)))
    up_weight = scatter_about(arg_keys[2], (D, FF), D ** -0.5, 0.078125, ((0, 4), (1, 8)))
    up_bias = scatter_about(arg_keys[3], (FF,), 0.5, 3.0, ((0, 8),))
    down_weight = scatter_about(arg_keys[4], (FF, D), FF ** -0.5, 0.0390625, ((0, 8), (1, 4)))
    return dict(normed=normed, out_grad=out_grad, up_weight=up_weight, up_bias=up_bias, down_weight=down_weight)


def gelu_parts(pre):
    cdf = 0.5 * (1.0 + jax.scipy.special.erf(pre / math.sqrt(2.0)))
    dens = jnp.exp(-0.5 * pre * pre) / math.sqrt(2.0 * math.pi)
    return (pre * cdf, cdf + pre * dens)

def reference(normed, out_grad, up_weight, up_bias, down_weight):
    pre = jnp.dot(normed, up_weight, preferred_element_type=jnp.float32) + up_bias.astype(jnp.float32)
    act, slope = gelu_parts(pre)
    hidden = act.astype(jnp.bfloat16)
    hidden_grad = jnp.dot(out_grad, down_weight.T, preferred_element_type=jnp.float32)
    pre_grad = (hidden_grad * slope).astype(jnp.bfloat16)
    up_grad = jnp.dot(normed.T, pre_grad, preferred_element_type=jnp.float32)
    bias_grad = lax.optimization_barrier(jnp.sum(pre_grad.astype(jnp.float32), axis=0))
    down_grad = jnp.dot(hidden.T, out_grad, preferred_element_type=jnp.float32)
    in_grad = jnp.dot(pre_grad, up_weight.T, preferred_element_type=jnp.float32).astype(jnp.bfloat16)
    return (in_grad, up_grad, bias_grad, down_grad)
```

```python
import functools
import math

import jax
import jax.numpy as jnp
from jax import lax
from jax.experimental import pallas as pl
from jax.experimental.pallas import tpu as pltpu
from jax.sharding import PartitionSpec as P

F32 = jnp.float32
BF16 = jnp.bfloat16
MIB = 1024 * 1024


def whole():
    return pl.BlockSpec(memory_space=pltpu.VMEM)


def call(kernel, out_shape, args, flops, nbytes, *, limit=24, grid=None, in_specs=None, out_specs=None, name=None):
    extra = {} if grid is None else {"grid": grid}
    return pl.pallas_call(
        kernel,
        out_shape=out_shape,
        in_specs=in_specs if in_specs is not None else [whole()] * len(args),
        out_specs=out_specs if out_specs is not None else jax.tree.map(lambda _: whole(), out_shape),
        compiler_params=pltpu.CompilerParams(vmem_limit_bytes=limit * MIB),
        cost_estimate=pl.CostEstimate(flops=flops, bytes_accessed=nbytes, transcendentals=0),
        name=name,
        **extra,
    )(*args)


def tree_sum(terms):
    while len(terms) > 1:
        terms = [terms[i] + terms[i + 1] for i in range(0, len(terms), 2)]
    return terms[0]


def divisor(size, most):
    tile = min(size, most)
    while size % tile:
        tile -= 128
    return tile


def core_of():
    return lax.rem(lax.axis_index("col"), 2)


def pre_kernel(core_ref, x_ref, w_ref, keep_ref, send_ref):
    core = core_ref[0]
    half = x_ref.shape[1]
    x = jnp.concatenate([x_ref[core], x_ref[1 - core]], axis=0)
    out = jnp.dot(x, w_ref[...], preferred_element_type=F32)
    keep_ref[...] = out[:half]
    send_ref[...] = out[half:].astype(BF16)


def hid_kernel(core_ref, g_ref, w_ref, keep_ref, send_ref):
    core = core_ref[0]
    half = g_ref.shape[1]
    g = jnp.concatenate([g_ref[core], g_ref[1 - core]], axis=0)
    out = lax.dot_general(g, w_ref[...], (((1,), (1,)), ((), ())), preferred_element_type=F32)
    keep_ref[...] = out[:half]
    send_ref[...] = out[half:].astype(BF16)


def add_kernel(a_ref, b_ref, o_ref):
    o_ref[...] = (a_ref[...] + b_ref[...].astype(F32)).astype(BF16)


def act_kernel(*refs):
    parts, bias_ref, act_ref, slope_ref = refs[:-3], refs[-3], refs[-2], refs[-1]
    pre = tree_sum([r[...].astype(F32) for r in parts]) + bias_ref[...].astype(F32)
    cdf = 0.5 * (1.0 + lax.erf(pre * (1.0 / math.sqrt(2.0))))
    dens = jnp.exp(-0.5 * pre * pre) * (1.0 / math.sqrt(2.0 * math.pi))
    act_ref[...] = (pre * cdf).astype(BF16)
    slope_ref[...] = cdf + pre * dens


def grad_kernel(*refs):
    parts, slope_ref, out_ref = refs[:-2], refs[-2], refs[-1]
    hid = tree_sum([r[...].astype(F32) for r in parts])
    out_ref[...] = (hid * slope_ref[...]).astype(BF16)


def down_kernel(core_ref, h0_ref, h1_ref, g_ref, out_ref):
    core = core_ref[0]
    g = jnp.concatenate([g_ref[core], g_ref[1 - core]], axis=0)
    h = jnp.concatenate([h0_ref[...], h1_ref[...]], axis=0)
    out_ref[...] = lax.dot_general(h, g, (((0,), (0,)), ((), ())), preferred_element_type=F32)


def up_kernel(core_ref, p0_ref, p1_ref, x_ref, out_ref):
    core = core_ref[0]
    x = jnp.concatenate([x_ref[core], x_ref[1 - core]], axis=0)
    p = jnp.concatenate([p0_ref[...], p1_ref[...]], axis=0)
    out_ref[...] = lax.dot_general(x, p, (((0,), (0,)), ((), ())), preferred_element_type=F32)


def in_kernel(core_ref, p0_ref, p1_ref, w_ref, keep_ref, send_ref, bias_ref):
    core = core_ref[0]
    half = p0_ref.shape[0]
    p = jnp.concatenate([p0_ref[...], p1_ref[...]], axis=0)
    out = lax.dot_general(p, w_ref[...], (((1,), (1,)), ((), ())), preferred_element_type=F32)
    own, other = out[:half], out[half:]
    near = core == 0
    keep_ref[...] = jnp.where(near, own, other)
    send_ref[...] = jnp.where(near, other, own).astype(BF16)

    @pl.when(pl.program_id(0) == 0)
    def _():
        own_sum = jnp.sum(p0_ref[...].astype(F32), axis=0, keepdims=True)
        other_sum = jnp.sum(p1_ref[...].astype(F32), axis=0, keepdims=True)
        bias_ref[...] = own_sum + other_sum


def on_device(rows, cols, normed, out_grad, up_weight, up_bias, down_weight):
    mine, feats = normed.shape
    units = up_weight.shape[1]
    half = mine * rows // 2
    core = core_of().astype(jnp.int32).reshape(1)
    smem = pl.BlockSpec(memory_space=pltpu.SMEM)

    def row_swap(x, k):
        return lax.ppermute(x, "row", [(i, i ^ k) for i in range(rows)])

    def col_swap(x, k):
        return lax.ppermute(x, "col", [(i, i ^ k) for i in range(cols)])

    stack = jnp.concatenate([normed, out_grad], axis=0)
    near = jnp.stack([stack] + [row_swap(stack, k) for k in range(2, rows, 2)])
    near = near.reshape(rows // 2, 2, mine, feats).transpose(1, 0, 2, 3).reshape(2, half, feats)
    far = row_swap(near, 1)
    inputs = jnp.stack([near[0], far[0]])
    grads = jnp.stack([near[1], far[1]])

    flops = 4 * half * feats * units
    wbytes = 2 * feats * units
    ft = divisor(units, 512)
    keep_t = jax.ShapeDtypeStruct((half, units), F32)
    send_t = jax.ShapeDtypeStruct((half, units), BF16)
    acts_spec = pl.BlockSpec((2, half, feats), lambda i: (0, 0, 0))
    unit_out = pl.BlockSpec((half, ft), lambda i: (0, i))
    keep_pre, send_pre = call(
        pre_kernel, (keep_t, send_t), (core, inputs, up_weight), flops, wbytes, grid=(units // ft,),
        in_specs=[smem, acts_spec, pl.BlockSpec((feats, ft), lambda i: (0, i))],
        out_specs=(unit_out, unit_out), name="pre",
    )
    other_pre = col_swap(send_pre, 1)
    keep_hid, send_hid = call(
        hid_kernel, (keep_t, send_t), (core, grads, down_weight), flops, wbytes, grid=(units // ft,),
        in_specs=[smem, acts_spec, pl.BlockSpec((ft, feats), lambda i: (i, 0))],
        out_specs=(unit_out, unit_out), name="hid",
    )
    other_hid = col_swap(send_hid, 1)

    chip_pre = call(add_kernel, send_t, (keep_pre, other_pre), half * units, 8 * half * units, name="add_pre")
    pre_parts = [chip_pre] + [col_swap(chip_pre, k) for k in range(2, cols, 2)]
    chip_hid = call(add_kernel, send_t, (keep_hid, other_hid), half * units, 8 * half * units, name="add_hid")
    hid_parts = [chip_hid] + [col_swap(chip_hid, k) for k in range(2, cols, 2)]

    act, slope = call(
        act_kernel, (send_t, keep_t), (*pre_parts, up_bias.reshape(1, units)), 20 * half * units, 10 * half * units, name="act"
    )
    act_far = col_swap(act, 1)
    pg = call(grad_kernel, send_t, (*hid_parts, slope), 3 * half * units, 8 * half * units, name="pre_grad")
    pg_far = col_swap(pg, 1)

    rt = divisor(units, 256)
    tok_block = pl.BlockSpec((half, rt), lambda i: (0, i))
    down_grad = call(
        down_kernel, jax.ShapeDtypeStruct((units, feats), F32), (core, act, act_far, grads), flops, 2 * wbytes,
        grid=(units // rt,), in_specs=[smem, tok_block, tok_block, acts_spec],
        out_specs=pl.BlockSpec((rt, feats), lambda i: (i, 0)), name="down_grad",
    )

    dt = divisor(feats, 256)
    whole_units = pl.BlockSpec((half, units), lambda i: (0, 0))
    feat_out = pl.BlockSpec((half, dt), lambda i: (0, i))
    keep_in, send_in, bias_grad = call(
        in_kernel,
        (
            jax.ShapeDtypeStruct((half, feats), F32),
            jax.ShapeDtypeStruct((half, feats), BF16),
            jax.ShapeDtypeStruct((1, units), F32),
        ),
        (core, pg, pg_far, up_weight), flops, wbytes, grid=(feats // dt,),
        in_specs=[smem, whole_units, whole_units, pl.BlockSpec((dt, units), lambda i: (i, 0))],
        out_specs=(feat_out, feat_out, pl.BlockSpec((1, units), lambda i: (0, 0))), name="in_part",
    )
    far_in = row_swap(send_in, 1)

    ut = divisor(feats, 128)
    up_grad = call(
        up_kernel, jax.ShapeDtypeStruct((feats, units), F32), (core, pg, pg_far, inputs), flops, 2 * wbytes,
        grid=(feats // ut,),
        in_specs=[smem, whole_units, whole_units, pl.BlockSpec((2, half, ut), lambda i: (0, 0, i))],
        out_specs=pl.BlockSpec((ut, units), lambda i: (i, 0)), name="up_grad",
    )

    share = (keep_in + far_in.astype(F32)).reshape(rows // 2, mine, feats)
    sends = share.astype(BF16)
    terms = [share[0]] + [row_swap(sends[k // 2], k).astype(F32) for k in range(2, rows, 2)]
    in_grad = tree_sum(terms).astype(BF16)
    return (in_grad, up_grad, bias_grad.reshape(units), down_grad)


def solution(mesh):
    in_specs = (P("row", "col"), P("row", "col"), P("col", "row"), P("row"), P("row", "col"))
    out_specs = (P("row", "col"), P("col", "row"), P("row"), P("row", "col"))
    body = functools.partial(on_device, mesh.shape["row"], mesh.shape["col"])
    return jax.shard_map(body, mesh=mesh, in_specs=in_specs, out_specs=out_specs, check_vma=False)
```

```python
import functools
import math

import jax
import jax.numpy as jnp
from jax import lax
from jax.experimental import pallas as pl
from jax.experimental.pallas import tpu as pltpu
from jax.sharding import PartitionSpec as P

F32 = jnp.float32
BF16 = jnp.bfloat16
MIB = 1024 * 1024
SLOTS = 4


def vmem():
    return pl.BlockSpec(memory_space=pltpu.VMEM)


def smem():
    return pl.BlockSpec(memory_space=pltpu.SMEM)


def anywhere():
    return pl.BlockSpec(memory_space=pl.ANY)


def call(kernel, name, out_shape, args, *, flops=0, nbytes=0, limit=16, in_specs=None, out_specs=None, scratch=(), aliases=None, after=()):
    in_specs = in_specs if in_specs is not None else [vmem()] * len(args)
    body = kernel
    if after:
        n, m = len(args), len(args) + len(after)

        def body(*refs):
            kernel(*refs[:n], *refs[m:])

    return pl.pallas_call(
        body,
        out_shape=out_shape,
        in_specs=in_specs + [anywhere()] * len(after),
        out_specs=out_specs if out_specs is not None else jax.tree.map(lambda _: vmem(), out_shape),
        scratch_shapes=list(scratch),
        input_output_aliases=aliases or {},
        compiler_params=pltpu.CompilerParams(vmem_limit_bytes=limit * MIB),
        cost_estimate=pl.CostEstimate(flops=0, bytes_accessed=0, transcendentals=0),
        name=name,
    )(*args, *after)


def tree_sum(terms):
    while len(terms) > 1:
        terms = [terms[i] + terms[i + 1] for i in range(0, len(terms), 2)]
    return terms[0]


def divisor(size, most):
    tile = min(size, most)
    while size % tile:
        tile -= 128
    return tile


def stack_kernel(a_ref, b_ref, o_ref, sems):
    copies = [pltpu.make_async_copy(r, o_ref.at[i], sems.at[i]) for i, r in enumerate((a_ref, b_ref))]
    for c in copies:
        c.start()
    for c in copies:
        c.wait()


def load_kernel(w_ref, o_ref, sem):
    copy = pltpu.make_async_copy(w_ref, o_ref, sem)
    copy.start()
    copy.wait()


def load(weight, name, limit, after=()):
    return call(
        load_kernel, name, pltpu.VMEM(weight.shape, weight.dtype), (weight,), nbytes=2 * weight.size, limit=limit,
        in_specs=[pl.BlockSpec(memory_space=pltpu.HBM)], out_specs=vmem(), scratch=[pltpu.SemaphoreType.DMA(())],
        after=after,
    )


def local_tokens(core, near_ref, far_ref):
    first = core == 0
    near, far = near_ref[...], far_ref[...]
    return jnp.concatenate([jnp.where(first, near, far), jnp.where(first, far, near)], axis=0)


def pre_kernel(core_ref, near_ref, far_ref, w_ref, keep_ref, send_ref):
    half, units = keep_ref.shape
    x = local_tokens(core_ref[0], near_ref, far_ref)
    tile = divisor(units, 512)
    for i in range(0, units, tile):
        out = jnp.dot(x, w_ref[:, i : i + tile], preferred_element_type=F32)
        keep_ref[:, i : i + tile] = out[:half]
        send_ref[:, i : i + tile] = out[half:]


def hid_kernel(start, core_ref, near_ref, far_ref, w_ref, keep_ref, send_ref):
    half, units = keep_ref.shape
    g = local_tokens(core_ref[0], near_ref, far_ref)
    tile = divisor(units, 512)
    for i in range(0, units, tile):
        w = w_ref[start + i : start + i + tile, :]
        out = lax.dot_general(w, g, (((1,), (1,)), ((), ())), preferred_element_type=F32).T
        keep_ref[:, i : i + tile] = out[:half]
        send_ref[:, i : i + tile] = out[half:]


def add_kernel(*refs):
    n, out_ref = len(refs) // 2, refs[-1]
    at = 0
    for a, b in zip(refs[:n], refs[n : 2 * n]):
        width = a.shape[1]
        out_ref[:, at : at + width] = (a[...] + b[...]).astype(BF16)
        at += width


def sum_kernel(a_ref, b_ref, out_ref):
    out_ref[...] = a_ref[...] + b_ref[...]


def act_kernel(*refs):
    parts, bias_ref, act_ref, slope_ref = refs[:-3], refs[-3], refs[-2], refs[-1]
    pre = tree_sum([r[...].astype(F32) for r in parts]) + bias_ref[...].astype(F32)
    cdf = 0.5 * (1.0 + lax.erf(pre * (1.0 / math.sqrt(2.0))))
    dens = jnp.exp(-0.5 * pre * pre) * (1.0 / math.sqrt(2.0 * math.pi))
    act_ref[...] = (pre * cdf).astype(BF16)
    slope_ref[...] = cdf + pre * dens


def grad_kernel(*refs):
    parts, slope_ref, out_ref = refs[:-2], refs[-2], refs[-1]
    hid = tree_sum([r[...].astype(F32) for r in parts])
    out_ref[...] = (hid * slope_ref[...]).astype(BF16)


def write_tiles(first, last, rows, make, out_ref, buf, sems, between=()):
    def copy(t):
        s = (t - first) % SLOTS
        return pltpu.make_async_copy(buf.at[s], out_ref.at[pl.ds(t * rows, rows), :], sems.at[s])

    work = list(between)
    count = last - first
    for t in range(first, last):
        if t - first >= SLOTS:
            copy(t - SLOTS).wait()
        buf[(t - first) % SLOTS] = make(t * rows)
        copy(t).start()
        left = len(between) * (last - 1 - t) // count
        while len(work) > left:
            work.pop(0)()
    for t in range(max(first, last - SLOTS), last):
        copy(t).wait()


def outer(a, b):
    return lax.dot_general(a, b, (((0,), (0,)), ((), ())), preferred_element_type=F32)


def down_kernel(first, last, rows, core_ref, h0_ref, h1_ref, near_ref, far_ref, *refs):
    out_ref, buf, sems = refs[-3:]
    g = local_tokens(core_ref[0], near_ref, far_ref)

    def make(at):
        return outer(jnp.concatenate([h0_ref[:, at : at + rows], h1_ref[:, at : at + rows]], axis=0), g)

    write_tiles(first, last, rows, make, out_ref, buf, sems)


def down_in_kernel(
    first, last, rows, core_ref, h0_ref, h1_ref, near_ref, far_ref, p0_ref, p1_ref, w_ref, _, out_ref, keep_ref, send_ref,
    bias_ref, buf, sems,
):
    near_first = core_ref[0] == 0
    g = local_tokens(core_ref[0], near_ref, far_ref)
    half = p0_ref.shape[0]
    p = jnp.concatenate([p0_ref[...], p1_ref[...]], axis=0)

    def make(at):
        return outer(jnp.concatenate([h0_ref[:, at : at + rows], h1_ref[:, at : at + rows]], axis=0), g)

    feats = w_ref.shape[0]
    tile = divisor(feats, 256)

    def part(i):
        w = w_ref[i : i + tile, :]
        out = lax.dot_general(w, p, (((1,), (1,)), ((), ())), preferred_element_type=F32).T
        own, other = out[:half], out[half:]
        keep_ref[:, i : i + tile] = jnp.where(near_first, own, other)
        send_ref[:, i : i + tile] = jnp.where(near_first, other, own)

    def bias():
        own = jnp.sum(p0_ref[...].astype(F32), axis=0, keepdims=True)
        bias_ref[...] = own + jnp.sum(p1_ref[...].astype(F32), axis=0, keepdims=True)

    work = [functools.partial(part, i) for i in range(0, feats, tile)] + [bias]
    write_tiles(first, last, rows, make, out_ref, buf, sems, work)


def up_kernel(first, last, rows, core_ref, p0_ref, p1_ref, near_ref, far_ref, *refs):
    out_ref, done_ref, buf, sems = refs[-4:]
    done_ref[...] = jnp.zeros_like(done_ref)
    p = local_tokens(core_ref[0], p0_ref, p1_ref)

    def make(at):
        return outer(jnp.concatenate([near_ref[:, at : at + rows], far_ref[:, at : at + rows]], axis=0), p)

    write_tiles(first, last, rows, make, out_ref, buf, sems)


def on_device(rows, cols, normed, out_grad, up_weight, up_bias, down_weight):
    mine, feats = normed.shape
    units = up_weight.shape[1]
    half = mine * rows // 2
    core = lax.rem(lax.axis_index("col"), 2).astype(jnp.int32).reshape(1)

    def row_swap(x, k):
        return lax.ppermute(x, "row", [(i, i ^ k) for i in range(rows)])

    def col_swap(x, k):
        return lax.ppermute(x, "col", [(i, i ^ k) for i in range(cols)])

    stack = call(
        stack_kernel, "stack", pltpu.VMEM((2, mine, feats), BF16), (normed, out_grad), nbytes=8 * mine * feats,
        in_specs=[anywhere()] * 2, out_specs=vmem(), scratch=[pltpu.SemaphoreType.DMA((2,))], limit=60,
    )
    near = jnp.stack([stack] + [row_swap(stack, k) for k in range(2, rows, 2)], axis=1)
    near = near.reshape(2, half, feats)
    far = row_swap(near, 1)
    w_up = load(up_weight, "load_up", 44)
    w_down = load(down_weight, "load_down", 38, (near,))

    flops = 4 * half * feats * units
    wbytes = 2 * feats * units
    keep_t = jax.ShapeDtypeStruct((half, units), F32)
    bf_t = jax.ShapeDtypeStruct((half, units), BF16)
    x_near, x_far, g_near, g_far = near[0], far[0], near[1], far[1]

    keep_pre, send_pre = call(
        pre_kernel, "pre", (keep_t, keep_t), (core, x_near, x_far, w_up), flops=flops, nbytes=wbytes,
        in_specs=[smem()] + [vmem()] * 3, after=(w_down,),
    )
    other_pre = col_swap(send_pre, 1)
    pieces = 2 if units % 256 == 0 else 1
    width = units // pieces
    piece_t = jax.ShapeDtypeStruct((half, width), F32)

    def hid_piece(i, after):
        return call(
            functools.partial(hid_kernel, i * width), "hid", (piece_t, piece_t), (core, g_near, g_far, w_down),
            flops=flops // pieces, nbytes=wbytes // pieces, in_specs=[smem()] + [vmem()] * 3, after=after,
        )

    hids = [hid_piece(0, ())]
    chip_pre = call(add_kernel, "add_pre", bf_t, (keep_pre, other_pre), nbytes=10 * half * units)
    pre_parts = [chip_pre] + [col_swap(chip_pre, k) for k in range(2, cols, 2)]
    hids += [hid_piece(i, (chip_pre,)) for i in range(1, pieces)]
    others = [col_swap(send, 1) for _, send in hids]
    chip_hid = call(add_kernel, "add_hid", bf_t, (*[k for k, _ in hids], *others), nbytes=10 * half * units)
    hid_parts = [chip_hid] + [col_swap(chip_hid, k) for k in range(2, cols, 2)]

    act, slope = call(act_kernel, "act", (bf_t, keep_t), (*pre_parts, up_bias.reshape(1, units)), nbytes=10 * half * units)
    act_far = col_swap(act, 1)
    pg = call(grad_kernel, "pre_grad", bf_t, (*hid_parts, slope), nbytes=10 * half * units)
    pg_far = col_swap(pg, 1)

    rt = divisor(units, 256)
    tiles = units // rt
    cut = tiles // 2
    down_t = jax.ShapeDtypeStruct((units, feats), F32)
    slots = [pltpu.VMEM((SLOTS, rt, feats), F32), pltpu.SemaphoreType.DMA((SLOTS,))]
    down_half = call(
        functools.partial(down_kernel, 0, cut, rt), "down_first", down_t, (core, act, act_far, g_near, g_far),
        flops=flops // 2, nbytes=wbytes, in_specs=[smem()] + [vmem()] * 4, out_specs=anywhere(), scratch=slots,
    )
    part_t = jax.ShapeDtypeStruct((half, feats), F32)
    down_grad, keep_in, send_in, bias_grad = call(
        functools.partial(down_in_kernel, cut, tiles, rt), "down_last_in",
        (down_t, part_t, part_t, jax.ShapeDtypeStruct((1, units), F32)),
        (core, act, act_far, g_near, g_far, pg, pg_far, w_up, down_half),
        flops=2 * flops, nbytes=2 * wbytes, in_specs=[smem()] + [vmem()] * 7 + [anywhere()],
        out_specs=(anywhere(), vmem(), vmem(), vmem()), scratch=slots, aliases={8: 0}, limit=24,
    )
    far_in = row_swap(send_in, 1)

    dt = divisor(feats, 128)
    dtiles = feats // dt
    dcut = dtiles // 2
    up_t = jax.ShapeDtypeStruct((feats, units), F32)
    slots = [pltpu.VMEM((SLOTS, dt, units), F32), pltpu.SemaphoreType.DMA((SLOTS,))]
    token_t = jax.ShapeDtypeStruct((8, 128), F32)
    up_half, wrote = call(
        functools.partial(up_kernel, 0, dcut, dt), "up_first", (up_t, token_t), (core, pg, pg_far, x_near, x_far),
        flops=flops // 2, nbytes=wbytes, in_specs=[smem()] + [vmem()] * 4, out_specs=(anywhere(), vmem()), scratch=slots,
    )
    share = call(sum_kernel, "share", part_t, (keep_in, far_in), nbytes=12 * half * feats, after=(wrote,))
    share = share.reshape(rows // 2, mine, feats)
    terms = [share[0]] + [row_swap(share[k // 2], k) for k in range(2, rows, 2)]
    up_grad, _ = call(
        functools.partial(up_kernel, dcut, dtiles, dt), "up_last", (up_t, token_t), (core, pg, pg_far, x_near, x_far, up_half),
        flops=flops // 2, nbytes=wbytes, in_specs=[smem()] + [vmem()] * 4 + [anywhere()], out_specs=(anywhere(), vmem()),
        scratch=slots, aliases={5: 0},
    )
    in_grad = tree_sum(terms).astype(BF16)
    return (in_grad, up_grad, bias_grad.reshape(units), down_grad)


def solution(mesh):
    in_specs = (P("row", "col"), P("row", "col"), P("col", "row"), P("row"), P("row", "col"))
    out_specs = (P("row", "col"), P("col", "row"), P("row"), P("row", "col"))
    body = functools.partial(on_device, mesh.shape["row"], mesh.shape["col"])
    return jax.shard_map(body, mesh=mesh, in_specs=in_specs, out_specs=out_specs, check_vma=False)
```

```python
import functools
import math

import jax
import jax.numpy as jnp
from jax import lax
from jax.experimental import pallas as pl
from jax.experimental.pallas import tpu as pltpu
from jax.sharding import PartitionSpec as P

F32 = jnp.float32
BF16 = jnp.bfloat16
MIB = 1024 * 1024
SLOTS = 4
EARLY = 16 * MIB
SCALE = 1000


def vmem():
    return pl.BlockSpec(memory_space=pltpu.VMEM)


def smem():
    return pl.BlockSpec(memory_space=pltpu.SMEM)


def anywhere():
    return pl.BlockSpec(memory_space=pl.ANY)


def call(kernel, name, out_shape, args, *, limit=16, in_specs=None, out_specs=None, scratch=(), aliases=None, after=(), cost=0):
    in_specs = in_specs if in_specs is not None else [vmem()] * len(args)
    body = kernel
    if after:
        n, m = len(args), len(args) + len(after)

        def body(*refs):
            kernel(*refs[:n], *refs[m:])

    return pl.pallas_call(
        body,
        out_shape=out_shape,
        in_specs=in_specs + [anywhere()] * len(after),
        out_specs=out_specs if out_specs is not None else jax.tree.map(lambda _: vmem(), out_shape),
        scratch_shapes=list(scratch),
        input_output_aliases=aliases or {},
        compiler_params=pltpu.CompilerParams(vmem_limit_bytes=limit * MIB),
        cost_estimate=pl.CostEstimate(flops=cost * SCALE, bytes_accessed=cost, transcendentals=0),
        name=name,
    )(*args, *after)


def tree_sum(terms):
    while len(terms) > 1:
        terms = [terms[i] + terms[i + 1] for i in range(0, len(terms), 2)]
    return terms[0]


def divisor(size, most):
    tile = min(size, most)
    while size % tile:
        tile -= 128
    return tile


def load_kernel(w_ref, o_ref, sem):
    copy = pltpu.make_async_copy(w_ref, o_ref, sem)
    copy.start()
    copy.wait()


def load(weight, name, limit, after):
    return call(
        load_kernel, name, pltpu.VMEM(weight.shape, weight.dtype), (weight,), limit=limit,
        in_specs=[anywhere()], out_specs=vmem(), scratch=[pltpu.SemaphoreType.DMA(())], after=after,
    )


def stack_kernel(a_ref, b_ref, o_ref, sems):
    copies = [pltpu.make_async_copy(r, o_ref.at[i], sems.at[i]) for i, r in enumerate((a_ref, b_ref))]
    for c in copies:
        c.start()
    for c in copies:
        c.wait()


def local_tokens(core, near_ref, far_ref):
    first = core == 0
    near, far = near_ref[...], far_ref[...]
    return jnp.concatenate([jnp.where(first, near, far), jnp.where(first, far, near)], axis=0)


def pre_kernel(core_ref, near_ref, far_ref, w_ref, keep_ref, send_ref):
    half, units = keep_ref.shape
    x = local_tokens(core_ref[0], near_ref, far_ref)
    tile = divisor(units, 512)
    for i in range(0, units, tile):
        out = jnp.dot(x, w_ref[:, i : i + tile], preferred_element_type=F32)
        keep_ref[:, i : i + tile] = out[:half]
        send_ref[:, i : i + tile] = out[half:]


def hid_kernel(start, core_ref, near_ref, far_ref, w_ref, keep_ref, send_ref):
    half, units = keep_ref.shape
    g = local_tokens(core_ref[0], near_ref, far_ref)
    tile = divisor(units, 512)
    for i in range(0, units, tile):
        w = w_ref[start + i : start + i + tile, :]
        out = lax.dot_general(w, g, (((1,), (1,)), ((), ())), preferred_element_type=F32).T
        keep_ref[:, i : i + tile] = out[:half]
        send_ref[:, i : i + tile] = out[half:]


def add_kernel(*refs):
    n, out_ref = len(refs) // 2, refs[-1]
    at = 0
    for a, b in zip(refs[:n], refs[n : 2 * n]):
        width = a.shape[1]
        out_ref[:, at : at + width] = (a[...] + b[...]).astype(BF16)
        at += width


def sum_kernel(a_ref, b_ref, out_ref):
    out_ref[...] = a_ref[...] + b_ref[...]


def act_kernel(*refs):
    parts, bias_ref, act_ref, slope_ref = refs[:-3], refs[-3], refs[-2], refs[-1]
    pre = tree_sum([r[...].astype(F32) for r in parts]) + bias_ref[...].astype(F32)
    cdf = 0.5 * (1.0 + lax.erf(pre * (1.0 / math.sqrt(2.0))))
    dens = jnp.exp(-0.5 * pre * pre) * (1.0 / math.sqrt(2.0 * math.pi))
    act_ref[...] = (pre * cdf).astype(BF16)
    slope_ref[...] = cdf + pre * dens


def grad_kernel(*refs):
    parts, slope_ref, out_ref = refs[:-2], refs[-2], refs[-1]
    hid = tree_sum([r[...].astype(F32) for r in parts])
    out_ref[...] = (hid * slope_ref[...]).astype(BF16)


def write_tiles(first, last, rows, make, out_ref, buf, sems):
    def copy(t):
        s = (t - first) % SLOTS
        return pltpu.make_async_copy(buf.at[s], out_ref.at[pl.ds(t * rows, rows), :], sems.at[s])

    for t in range(first, last):
        if t - first >= SLOTS:
            copy(t - SLOTS).wait()
        buf[(t - first) % SLOTS] = make(t * rows)
        copy(t).start()
    for t in range(max(first, last - SLOTS), last):
        copy(t).wait()


def outer(a, b):
    return lax.dot_general(a, b, (((0,), (0,)), ((), ())), preferred_element_type=F32)


def down_kernel(first, last, rows, core_ref, h0_ref, h1_ref, near_ref, far_ref, *refs):
    out_ref, done_ref, buf, sems = refs[-4:]
    done_ref[...] = jnp.zeros_like(done_ref)
    g = local_tokens(core_ref[0], near_ref, far_ref)

    def make(at):
        return outer(jnp.concatenate([h0_ref[:, at : at + rows], h1_ref[:, at : at + rows]], axis=0), g)

    write_tiles(first, last, rows, make, out_ref, buf, sems)


def in_kernel(core_ref, p0_ref, p1_ref, w_ref, keep_ref, send_ref, bias_ref):
    near_first = core_ref[0] == 0
    half = p0_ref.shape[0]
    p0, p1 = p0_ref[...], p1_ref[...]
    p = jnp.concatenate([jnp.where(near_first, p0, p1), jnp.where(near_first, p1, p0)], axis=0)
    feats = w_ref.shape[0]
    tile = divisor(feats, 512)
    for i in range(0, feats, tile):
        out = lax.dot_general(w_ref[i : i + tile, :], p, (((1,), (1,)), ((), ())), preferred_element_type=F32).T
        keep_ref[:, i : i + tile] = out[:half]
        send_ref[:, i : i + tile] = out[half:]
    own = jnp.sum(p0.astype(F32), axis=0, keepdims=True)
    bias_ref[...] = own + jnp.sum(p1.astype(F32), axis=0, keepdims=True)


def up_kernel(first, last, rows, core_ref, p0_ref, p1_ref, near_ref, far_ref, *refs):
    out_ref, done_ref, buf, sems = refs[-4:]
    done_ref[...] = jnp.zeros_like(done_ref)
    p = local_tokens(core_ref[0], p0_ref, p1_ref)

    def make(at):
        return outer(jnp.concatenate([near_ref[:, at : at + rows], far_ref[:, at : at + rows]], axis=0), p)

    write_tiles(first, last, rows, make, out_ref, buf, sems)


def on_device(rows, cols, normed, out_grad, up_weight, up_bias, down_weight):
    mine, feats = normed.shape
    units = up_weight.shape[1]
    half = mine * rows // 2
    core = lax.rem(lax.axis_index("col"), 2).astype(jnp.int32).reshape(1)

    def row_swap(x, k):
        return lax.ppermute(x, "row", [(i, i ^ k) for i in range(rows)])

    def col_swap(x, k):
        return lax.ppermute(x, "col", [(i, i ^ k) for i in range(cols)])

    blocks = rows // 2
    stack = call(
        stack_kernel, "stack", pltpu.VMEM((2, mine, feats), BF16), (normed, out_grad),
        in_specs=[anywhere()] * 2, out_specs=vmem(), scratch=[pltpu.SemaphoreType.DMA((2,))], limit=58,
    )
    near = jnp.stack([stack] + [row_swap(stack, k) for k in range(2, rows, 2)], axis=1)
    near = near.reshape(2, half, feats)
    far = row_swap(near, 1)
    up_weight = load(up_weight, "load_up", 44, ())
    down_weight = load(down_weight, "load_down", 38, (near,))
    x_near, x_far, g_near, g_far = near[0], far[0], near[1], far[1]

    keep_t = jax.ShapeDtypeStruct((half, units), F32)
    bf_t = jax.ShapeDtypeStruct((half, units), BF16)
    keep_pre, send_pre = call(
        pre_kernel, "pre", (keep_t, keep_t), (core, x_near, x_far, up_weight), in_specs=[smem()] + [vmem()] * 3,
        after=(down_weight,),
    )
    other_pre = col_swap(send_pre, 1)

    cut = units * 2 // 3 // 128 * 128

    def hid_piece(start, width, after):
        piece_t = jax.ShapeDtypeStruct((half, width), F32)
        return call(
            functools.partial(hid_kernel, start), "hid", (piece_t, piece_t), (core, g_near, g_far, down_weight),
            in_specs=[smem()] + [vmem()] * 3, after=after,
        )

    hids = [hid_piece(0, cut, ())]
    chip_pre = call(add_kernel, "add_pre", bf_t, (keep_pre, other_pre), after=(hids[0][1],), cost=EARLY)
    pre_parts = [chip_pre] + [col_swap(chip_pre, k) for k in range(2, cols, 2)]
    hids.append(hid_piece(cut, units - cut, (chip_pre,)))
    act, slope = call(act_kernel, "act", (bf_t, keep_t), (*pre_parts, up_bias.reshape(1, units)), cost=EARLY)
    act_far = col_swap(act, 1)
    others = [col_swap(send, 1) for _, send in hids]
    chip_hid = call(add_kernel, "add_hid", bf_t, (*[k for k, _ in hids], *others))
    hid_parts = [chip_hid] + [col_swap(chip_hid, k) for k in range(2, cols, 2)]
    pg = call(grad_kernel, "pre_grad", bf_t, (*hid_parts, slope), after=(act_far,))
    pg_far = col_swap(pg, 1)

    part_t = jax.ShapeDtypeStruct((half, feats), F32)
    token_t = jax.ShapeDtypeStruct((8, 128), F32)
    keep_in, send_in, bias_grad = call(
        in_kernel, "in_part", (part_t, part_t, jax.ShapeDtypeStruct((1, units), F32)), (core, pg, pg_far, up_weight),
        in_specs=[smem()] + [vmem()] * 3,
    )
    far_in = row_swap(send_in, 1)

    rt = divisor(units, 256)
    down_grad, wrote = call(
        functools.partial(down_kernel, 0, units // rt, rt), "down_grad",
        (jax.ShapeDtypeStruct((units, feats), F32), token_t), (core, act, act_far, g_near, g_far),
        in_specs=[smem()] + [vmem()] * 4, out_specs=(anywhere(), vmem()),
        scratch=[pltpu.VMEM((SLOTS, rt, feats), F32), pltpu.SemaphoreType.DMA((SLOTS,))], after=(send_in,),
    )
    share = call(sum_kernel, "share", part_t, (keep_in, far_in), after=(wrote,)).reshape(blocks, mine, feats)
    terms = [share[0]] + [row_swap(share[k // 2], k) for k in range(2, rows, 2)]

    dt = divisor(feats, 128)
    up_grad, _ = call(
        functools.partial(up_kernel, 0, feats // dt, dt), "up_grad",
        (jax.ShapeDtypeStruct((feats, units), F32), token_t), (core, pg, pg_far, x_near, x_far),
        in_specs=[smem()] + [vmem()] * 4, out_specs=(anywhere(), vmem()),
        scratch=[pltpu.VMEM((SLOTS, dt, units), F32), pltpu.SemaphoreType.DMA((SLOTS,))], after=(share,),
    )
    in_grad = tree_sum(terms).astype(BF16)
    return (in_grad, up_grad, bias_grad.reshape(units), down_grad)


def solution(mesh):
    in_specs = (P("row", "col"), P("row", "col"), P("col", "row"), P("row"), P("row", "col"))
    out_specs = (P("row", "col"), P("col", "row"), P("row"), P("row", "col"))
    body = functools.partial(on_device, mesh.shape["row"], mesh.shape["col"])
    return jax.shard_map(body, mesh=mesh, in_specs=in_specs, out_specs=out_specs, check_vma=False)
```

```python
import functools
import math

import jax
import jax.numpy as jnp
from jax import lax
from jax.experimental import pallas as pl
from jax.experimental.pallas import tpu as pltpu
from jax.sharding import PartitionSpec as P

F32 = jnp.float32
BF16 = jnp.bfloat16
MIB = 1024 * 1024
SLOTS = 4
DOWN_EARLY = 8
EARLY = 16 * MIB
SCALE = 1000


def vmem():
    return pl.BlockSpec(memory_space=pltpu.VMEM)


def smem():
    return pl.BlockSpec(memory_space=pltpu.SMEM)


def anywhere():
    return pl.BlockSpec(memory_space=pl.ANY)


def call(kernel, name, out_shape, args, *, limit=16, in_specs=None, out_specs=None, scratch=(), aliases=None, after=(), cost=0):
    in_specs = in_specs if in_specs is not None else [vmem()] * len(args)
    body = kernel
    if after:
        n, m = len(args), len(args) + len(after)

        def body(*refs):
            kernel(*refs[:n], *refs[m:])

    return pl.pallas_call(
        body,
        out_shape=out_shape,
        in_specs=in_specs + [anywhere()] * len(after),
        out_specs=out_specs if out_specs is not None else jax.tree.map(lambda _: vmem(), out_shape),
        scratch_shapes=list(scratch),
        input_output_aliases=aliases or {},
        compiler_params=pltpu.CompilerParams(vmem_limit_bytes=limit * MIB),
        cost_estimate=pl.CostEstimate(flops=cost * SCALE, bytes_accessed=cost, transcendentals=0),
        name=name,
    )(*args, *after)


def tree_sum(terms):
    while len(terms) > 1:
        terms = [terms[i] + terms[i + 1] for i in range(0, len(terms), 2)]
    return terms[0]


def divisor(size, most):
    tile = min(size, most)
    while size % tile:
        tile -= 128
    return tile


def load_kernel(w_ref, o_ref, sem):
    copy = pltpu.make_async_copy(w_ref, o_ref, sem)
    copy.start()
    copy.wait()


def load(weight, name, limit, after):
    return call(
        load_kernel, name, pltpu.VMEM(weight.shape, weight.dtype), (weight,), limit=limit,
        in_specs=[anywhere()], out_specs=vmem(), scratch=[pltpu.SemaphoreType.DMA(())], after=after,
    )


def stack_kernel(a_ref, b_ref, o_ref, sems):
    copies = [pltpu.make_async_copy(r, o_ref.at[i], sems.at[i]) for i, r in enumerate((a_ref, b_ref))]
    for c in copies:
        c.start()
    for c in copies:
        c.wait()


def local_tokens(core, near_ref, far_ref):
    first = core == 0
    near, far = near_ref[...], far_ref[...]
    return jnp.concatenate([jnp.where(first, near, far), jnp.where(first, far, near)], axis=0)


def pre_kernel(core_ref, near_ref, far_ref, w_ref, keep_ref, send_ref):
    half, units = keep_ref.shape
    x = local_tokens(core_ref[0], near_ref, far_ref)
    tile = divisor(units, 512)
    for i in range(0, units, tile):
        out = jnp.dot(x, w_ref[:, i : i + tile], preferred_element_type=F32)
        keep_ref[:, i : i + tile] = out[:half]
        send_ref[:, i : i + tile] = out[half:]


def hid_kernel(start, core_ref, near_ref, far_ref, w_ref, keep_ref, send_ref):
    half, units = keep_ref.shape
    g = local_tokens(core_ref[0], near_ref, far_ref)
    tile = divisor(units, 512)
    for i in range(0, units, tile):
        w = w_ref[start + i : start + i + tile, :]
        out = lax.dot_general(w, g, (((1,), (1,)), ((), ())), preferred_element_type=F32).T
        keep_ref[:, i : i + tile] = out[:half]
        send_ref[:, i : i + tile] = out[half:]


def add_kernel(*refs):
    n, out_ref = len(refs) // 2, refs[-1]
    at = 0
    for a, b in zip(refs[:n], refs[n : 2 * n]):
        width = a.shape[1]
        out_ref[:, at : at + width] = (a[...] + b[...]).astype(BF16)
        at += width


def sum_kernel(a_ref, b_ref, out_ref):
    out_ref[...] = a_ref[...] + b_ref[...].astype(F32)


def act_kernel(*refs):
    parts, bias_ref, act_ref, slope_ref = refs[:-3], refs[-3], refs[-2], refs[-1]
    pre = tree_sum([r[...].astype(F32) for r in parts]) + bias_ref[...].astype(F32)
    cdf = 0.5 * (1.0 + lax.erf(pre * (1.0 / math.sqrt(2.0))))
    dens = jnp.exp(-0.5 * pre * pre) * (1.0 / math.sqrt(2.0 * math.pi))
    act_ref[...] = (pre * cdf).astype(BF16)
    slope_ref[...] = cdf + pre * dens


def grad_kernel(*refs):
    parts, slope_ref, out_ref = refs[:-2], refs[-2], refs[-1]
    hid = tree_sum([r[...].astype(F32) for r in parts])
    out_ref[...] = (hid * slope_ref[...]).astype(BF16)


def write_tiles(first, last, rows, make, out_ref, buf, sems):
    def copy(t):
        s = (t - first) % SLOTS
        return pltpu.make_async_copy(buf.at[s], out_ref.at[pl.ds(t * rows, rows), :], sems.at[s])

    for t in range(first, last):
        if t - first >= SLOTS:
            copy(t - SLOTS).wait()
        buf[(t - first) % SLOTS] = make(t * rows)
        copy(t).start()
    for t in range(max(first, last - SLOTS), last):
        copy(t).wait()


def outer(a, b):
    return lax.dot_general(a, b, (((0,), (0,)), ((), ())), preferred_element_type=F32)


def down_kernel(first, last, rows, core_ref, h0_ref, h1_ref, near_ref, far_ref, *refs):
    out_ref, done_ref, buf, sems = refs[-4:]
    done_ref[...] = jnp.zeros_like(done_ref)
    g = local_tokens(core_ref[0], near_ref, far_ref)

    def make(at):
        return outer(jnp.concatenate([h0_ref[:, at : at + rows], h1_ref[:, at : at + rows]], axis=0), g)

    write_tiles(first, last, rows, make, out_ref, buf, sems)


def down_in_kernel(
    last, rows, core_ref, p0_ref, p1_ref, w_ref, h0_ref, h1_ref, near_ref, far_ref, out_ref, keep_ref, send_ref, bias_ref, p_ref,
    buf, sems,
):
    near_first = core_ref[0] == 0
    g = local_tokens(core_ref[0], near_ref, far_ref)
    copies = [
        pltpu.make_async_copy(buf.at[t], out_ref.at[pl.ds(t * rows, rows), :], sems.at[t]) for t in range(last)
    ]
    for t in range(last):
        at = t * rows
        buf[t] = outer(jnp.concatenate([h0_ref[:, at : at + rows], h1_ref[:, at : at + rows]], axis=0), g)
        copies[t].start()
    half = p0_ref.shape[0]
    p0, p1 = p0_ref[...], p1_ref[...]
    p = jnp.concatenate([jnp.where(near_first, p0, p1), jnp.where(near_first, p1, p0)], axis=0)
    p_ref[...] = p
    feats = w_ref.shape[0]
    tile = divisor(feats, 512)
    for i in range(0, feats, tile):
        out = lax.dot_general(w_ref[i : i + tile, :], p, (((1,), (1,)), ((), ())), preferred_element_type=F32).T
        keep_ref[:, i : i + tile] = out[:half]
        send_ref[:, i : i + tile] = out[half:].astype(BF16)
    own = jnp.sum(p0.astype(F32), axis=0, keepdims=True)
    bias_ref[...] = own + jnp.sum(p1.astype(F32), axis=0, keepdims=True)
    for t in range(last):
        copies[t].wait()


def up_kernel(rows, p_ref, near_ref, far_ref, out_ref, buf, sems):
    p = p_ref[...]

    def make(at):
        return outer(jnp.concatenate([near_ref[:, at : at + rows], far_ref[:, at : at + rows]], axis=0), p)

    write_tiles(0, out_ref.shape[0] // rows, rows, make, out_ref, buf, sems)


def on_device(rows, cols, normed, out_grad, up_weight, up_bias, down_weight):
    mine, feats = normed.shape
    units = up_weight.shape[1]
    half = mine * rows // 2
    core = lax.rem(lax.axis_index("col"), 2).astype(jnp.int32).reshape(1)

    def row_swap(x, k):
        return lax.ppermute(x, "row", [(i, i ^ k) for i in range(rows)])

    def col_swap(x, k):
        return lax.ppermute(x, "col", [(i, i ^ k) for i in range(cols)])

    blocks = rows // 2
    stack = call(
        stack_kernel, "stack", pltpu.VMEM((2, mine, feats), BF16), (normed, out_grad),
        in_specs=[anywhere()] * 2, out_specs=vmem(), scratch=[pltpu.SemaphoreType.DMA((2,))], limit=58,
    )
    near = jnp.stack([stack] + [row_swap(stack, k) for k in range(2, rows, 2)], axis=1)
    near = near.reshape(2, half, feats)
    far = row_swap(near, 1)
    up_weight = load(up_weight, "load_up", 44, ())
    down_weight = load(down_weight, "load_down", 38, (near,))
    x_near, x_far, g_near, g_far = near[0], far[0], near[1], far[1]

    keep_t = jax.ShapeDtypeStruct((half, units), F32)
    bf_t = jax.ShapeDtypeStruct((half, units), BF16)
    keep_pre, send_pre = call(
        pre_kernel, "pre", (keep_t, keep_t), (core, x_near, x_far, up_weight), in_specs=[smem()] + [vmem()] * 3,
        after=(down_weight,),
    )
    other_pre = col_swap(send_pre, 1)

    cut = units * 2 // 3 // 128 * 128

    def hid_piece(start, width, after):
        piece_t = jax.ShapeDtypeStruct((half, width), F32)
        return call(
            functools.partial(hid_kernel, start), "hid", (piece_t, piece_t), (core, g_near, g_far, down_weight),
            in_specs=[smem()] + [vmem()] * 3, after=after,
        )

    hids = [hid_piece(0, cut, ())]
    chip_pre = call(add_kernel, "add_pre", bf_t, (keep_pre, other_pre), after=(hids[0][1],), cost=EARLY)
    pre_parts = [chip_pre] + [col_swap(chip_pre, k) for k in range(2, cols, 2)]
    hids.append(hid_piece(cut, units - cut, (chip_pre,)))
    act, slope = call(act_kernel, "act", (bf_t, keep_t), (*pre_parts, up_bias.reshape(1, units)), cost=EARLY)
    act_far = col_swap(act, 1)
    others = [col_swap(send, 1) for _, send in hids]
    chip_hid = call(add_kernel, "add_hid", bf_t, (*[k for k, _ in hids], *others))
    hid_parts = [chip_hid] + [col_swap(chip_hid, k) for k in range(2, cols, 2)]
    pg = call(grad_kernel, "pre_grad", bf_t, (*hid_parts, slope), after=(act_far,))
    pg_far = col_swap(pg, 1)

    rt = divisor(units, 256)
    tiles = units // rt
    early = max(1, tiles * DOWN_EARLY // 12)
    part_t = jax.ShapeDtypeStruct((half, feats), F32)
    token_t = jax.ShapeDtypeStruct((8, 128), F32)
    down_t = jax.ShapeDtypeStruct((units, feats), F32)
    down_early, keep_in, send_in, bias_grad, pg_all = call(
        functools.partial(down_in_kernel, early, rt), "down_in",
        (down_t, part_t, jax.ShapeDtypeStruct((half, feats), BF16), jax.ShapeDtypeStruct((1, units), F32), jax.ShapeDtypeStruct((2 * half, units), BF16)),
        (core, pg, pg_far, up_weight, act, act_far, g_near, g_far), in_specs=[smem()] + [vmem()] * 7,
        out_specs=(anywhere(),) + (vmem(),) * 4, limit=24,
        scratch=[pltpu.VMEM((early, rt, feats), F32), pltpu.SemaphoreType.DMA((early,))],
    )
    far_in = row_swap(send_in, 1)

    down_grad, wrote = call(
        functools.partial(down_kernel, early, tiles, rt), "down_grad", (down_t, token_t),
        (core, act, act_far, g_near, g_far, down_early), in_specs=[smem()] + [vmem()] * 4 + [anywhere()],
        out_specs=(anywhere(), vmem()), scratch=[pltpu.VMEM((SLOTS, rt, feats), F32), pltpu.SemaphoreType.DMA((SLOTS,))],
        aliases={5: 0}, after=(send_in,),
    )
    share = call(sum_kernel, "share", part_t, (keep_in, far_in), after=(wrote,)).reshape(blocks, mine, feats)
    terms = [share[0]] + [row_swap(share[k // 2], k) for k in range(2, rows, 2)]

    dt = divisor(feats, 128)
    up_grad = call(
        functools.partial(up_kernel, dt), "up_grad", jax.ShapeDtypeStruct((feats, units), F32), (pg_all, x_near, x_far),
        in_specs=[vmem()] * 3, out_specs=anywhere(),
        scratch=[pltpu.VMEM((SLOTS, dt, units), F32), pltpu.SemaphoreType.DMA((SLOTS,))], after=(share,),
    )
    in_grad = tree_sum(terms).astype(BF16)
    return (in_grad, up_grad, bias_grad.reshape(units), down_grad)


def solution(mesh):
    in_specs = (P("row", "col"), P("row", "col"), P("col", "row"), P("row"), P("row", "col"))
    out_specs = (P("row", "col"), P("col", "row"), P("row"), P("row", "col"))
    body = functools.partial(on_device, mesh.shape["row"], mesh.shape["col"])
    return jax.shard_map(body, mesh=mesh, in_specs=in_specs, out_specs=out_specs, check_vma=False)
```

```python
import functools
import math

import jax
import jax.numpy as jnp
from jax import lax
from jax.experimental import pallas as pl
from jax.experimental.pallas import tpu as pltpu
from jax.sharding import PartitionSpec as P

F32 = jnp.float32
BF16 = jnp.bfloat16
MIB = 1024 * 1024
SLOTS = 4
UP_FIRST = 4
EARLY = 16 * MIB
SCALE = 1000


def vmem():
    return pl.BlockSpec(memory_space=pltpu.VMEM)


def smem():
    return pl.BlockSpec(memory_space=pltpu.SMEM)


def anywhere():
    return pl.BlockSpec(memory_space=pl.ANY)


def call(kernel, name, out_shape, args, *, limit=16, in_specs=None, out_specs=None, scratch=(), aliases=None, after=(), cost=0):
    in_specs = in_specs if in_specs is not None else [vmem()] * len(args)
    body = kernel
    if after:
        n, m = len(args), len(args) + len(after)

        def body(*refs):
            kernel(*refs[:n], *refs[m:])

    return pl.pallas_call(
        body,
        out_shape=out_shape,
        in_specs=in_specs + [anywhere()] * len(after),
        out_specs=out_specs if out_specs is not None else jax.tree.map(lambda _: vmem(), out_shape),
        scratch_shapes=list(scratch),
        input_output_aliases=aliases or {},
        compiler_params=pltpu.CompilerParams(vmem_limit_bytes=limit * MIB),
        cost_estimate=pl.CostEstimate(flops=cost * SCALE, bytes_accessed=cost, transcendentals=0),
        name=name,
    )(*args, *after)


def tree_sum(terms):
    while len(terms) > 1:
        terms = [terms[i] + terms[i + 1] for i in range(0, len(terms), 2)]
    return terms[0]


def divisor(size, most):
    tile = min(size, most)
    while size % tile:
        tile -= 128
    return tile


def load_kernel(w_ref, o_ref, sem):
    copy = pltpu.make_async_copy(w_ref, o_ref, sem)
    copy.start()
    copy.wait()


def load(weight, name, limit, after):
    return call(
        load_kernel, name, pltpu.VMEM(weight.shape, weight.dtype), (weight,), limit=limit,
        in_specs=[anywhere()], out_specs=vmem(), scratch=[pltpu.SemaphoreType.DMA(())], after=after,
    )


def stack_kernel(a_ref, b_ref, o_ref, sems):
    copies = [pltpu.make_async_copy(r, o_ref.at[i], sems.at[i]) for i, r in enumerate((a_ref, b_ref))]
    for c in copies:
        c.start()
    for c in copies:
        c.wait()


def local_tokens(core, near_ref, far_ref):
    first = core == 0
    near, far = near_ref[...], far_ref[...]
    return jnp.concatenate([jnp.where(first, near, far), jnp.where(first, far, near)], axis=0)


def pre_kernel(core_ref, near_ref, far_ref, w_ref, keep_ref, send_ref):
    half, units = keep_ref.shape
    x = local_tokens(core_ref[0], near_ref, far_ref)
    tile = divisor(units, 512)
    for i in range(0, units, tile):
        out = jnp.dot(x, w_ref[:, i : i + tile], preferred_element_type=F32)
        keep_ref[:, i : i + tile] = out[:half]
        send_ref[:, i : i + tile] = out[half:]


def hid_kernel(start, core_ref, near_ref, far_ref, w_ref, keep_ref, send_ref):
    half, units = keep_ref.shape
    g = local_tokens(core_ref[0], near_ref, far_ref)
    tile = divisor(units, 512)
    for i in range(0, units, tile):
        w = w_ref[start + i : start + i + tile, :]
        out = lax.dot_general(w, g, (((1,), (1,)), ((), ())), preferred_element_type=F32).T
        keep_ref[:, i : i + tile] = out[:half]
        send_ref[:, i : i + tile] = out[half:]


def add_kernel(*refs):
    n, out_ref = len(refs) // 2, refs[-1]
    at = 0
    for a, b in zip(refs[:n], refs[n : 2 * n]):
        width = a.shape[1]
        out_ref[:, at : at + width] = (a[...] + b[...]).astype(BF16)
        at += width


def add_cut_kernel(cut, a_ref, b_ref, first_ref, second_ref):
    total = (a_ref[...] + b_ref[...]).astype(BF16)
    first_ref[...] = total[:, :cut]
    second_ref[...] = total[:, cut:]


def sum_kernel(a_ref, b_ref, out_ref):
    out_ref[...] = a_ref[...] + b_ref[...].astype(F32)


def act_kernel(start, *refs):
    parts, bias_ref, act_ref, slope_ref = refs[:-3], refs[-3], refs[-2], refs[-1]
    bias = bias_ref[:, start : start + act_ref.shape[1]].astype(F32)
    pre = tree_sum([r[...].astype(F32) for r in parts]) + bias
    cdf = 0.5 * (1.0 + lax.erf(pre * (1.0 / math.sqrt(2.0))))
    dens = jnp.exp(-0.5 * pre * pre) * (1.0 / math.sqrt(2.0 * math.pi))
    act_ref[...] = (pre * cdf).astype(BF16)
    slope_ref[...] = cdf + pre * dens


def grad_kernel(cut, *refs):
    parts, (slope_a, slope_b, out_ref) = refs[:-3], refs[-3:]
    hid = tree_sum([r[...].astype(F32) for r in parts])
    out_ref[:, :cut] = (hid[:, :cut] * slope_a[...]).astype(BF16)
    out_ref[:, cut:] = (hid[:, cut:] * slope_b[...]).astype(BF16)


def write_tiles(first, last, rows, make, out_ref, buf, sems):
    def copy(t):
        s = (t - first) % SLOTS
        return pltpu.make_async_copy(buf.at[s], out_ref.at[pl.ds(t * rows, rows), :], sems.at[s])

    for t in range(first, last):
        if t - first >= SLOTS:
            copy(t - SLOTS).wait()
        buf[(t - first) % SLOTS] = make(t * rows)
        copy(t).start()
    for t in range(max(first, last - SLOTS), last):
        copy(t).wait()


def outer(a, b):
    return lax.dot_general(a, b, (((0,), (0,)), ((), ())), preferred_element_type=F32)


def down_kernel(first, last, rows, core_ref, h0_ref, h1_ref, near_ref, far_ref, *refs):
    out_ref, done_ref, buf, sems = refs[-4:]
    done_ref[...] = jnp.zeros_like(done_ref)
    g = local_tokens(core_ref[0], near_ref, far_ref)

    def make(at):
        return outer(jnp.concatenate([h0_ref[:, at : at + rows], h1_ref[:, at : at + rows]], axis=0), g)

    write_tiles(first, last, rows, make, out_ref, buf, sems)


def down_in_kernel(
    base, last, rows, core_ref, p0_ref, p1_ref, w_ref, h0_ref, h1_ref, near_ref, far_ref, _, out_ref, keep_ref, send_ref, bias_ref, p_ref,
    buf, sems,
):
    near_first = core_ref[0] == 0
    g = local_tokens(core_ref[0], near_ref, far_ref)
    copies = [
        pltpu.make_async_copy(buf.at[t], out_ref.at[pl.ds(base + t * rows, rows), :], sems.at[t]) for t in range(last)
    ]
    for t in range(last):
        at = t * rows
        buf[t] = outer(jnp.concatenate([h0_ref[:, at : at + rows], h1_ref[:, at : at + rows]], axis=0), g)
        copies[t].start()
    half = p0_ref.shape[0]
    p0, p1 = p0_ref[...], p1_ref[...]
    p = jnp.concatenate([jnp.where(near_first, p0, p1), jnp.where(near_first, p1, p0)], axis=0)
    p_ref[...] = p
    feats = w_ref.shape[0]
    tile = divisor(feats, 512)
    for i in range(0, feats, tile):
        out = lax.dot_general(w_ref[i : i + tile, :], p, (((1,), (1,)), ((), ())), preferred_element_type=F32).T
        keep_ref[:, i : i + tile] = out[:half]
        send_ref[:, i : i + tile] = out[half:].astype(BF16)
    own = jnp.sum(p0.astype(F32), axis=0, keepdims=True)
    bias_ref[...] = own + jnp.sum(p1.astype(F32), axis=0, keepdims=True)
    for t in range(last):
        copies[t].wait()


def up_kernel(first, last, rows, p_ref, near_ref, far_ref, *refs):
    out_ref, done_ref, buf, sems = refs[-4:]
    done_ref[...] = jnp.zeros_like(done_ref)
    p = p_ref[...]

    def make(at):
        return outer(jnp.concatenate([near_ref[:, at : at + rows], far_ref[:, at : at + rows]], axis=0), p)

    write_tiles(first, last, rows, make, out_ref, buf, sems)


def on_device(rows, cols, normed, out_grad, up_weight, up_bias, down_weight):
    mine, feats = normed.shape
    units = up_weight.shape[1]
    half = mine * rows // 2
    core = lax.rem(lax.axis_index("col"), 2).astype(jnp.int32).reshape(1)

    def row_swap(x, k):
        return lax.ppermute(x, "row", [(i, i ^ k) for i in range(rows)])

    def col_swap(x, k):
        return lax.ppermute(x, "col", [(i, i ^ k) for i in range(cols)])

    blocks = rows // 2
    stack = call(
        stack_kernel, "stack", pltpu.VMEM((2, mine, feats), BF16), (normed, out_grad),
        in_specs=[anywhere()] * 2, out_specs=vmem(), scratch=[pltpu.SemaphoreType.DMA((2,))], limit=58,
    )
    near = jnp.stack([stack] + [row_swap(stack, k) for k in range(2, rows, 2)], axis=1)
    near = near.reshape(2, half, feats)
    far = row_swap(near, 1)
    up_weight = load(up_weight, "load_up", 44, ())
    down_weight = load(down_weight, "load_down", 38, (near,))
    x_near, x_far, g_near, g_far = near[0], far[0], near[1], far[1]

    keep_t = jax.ShapeDtypeStruct((half, units), F32)
    bf_t = jax.ShapeDtypeStruct((half, units), BF16)
    keep_pre, send_pre = call(
        pre_kernel, "pre", (keep_t, keep_t), (core, x_near, x_far, up_weight), in_specs=[smem()] + [vmem()] * 3,
        after=(down_weight,),
    )
    other_pre = col_swap(send_pre, 1)

    part = units * 2 // 3 // 128 * 128
    cut = units // 2 // 128 * 128

    def hid_piece(start, width, after):
        piece_t = jax.ShapeDtypeStruct((half, width), F32)
        return call(
            functools.partial(hid_kernel, start), "hid", (piece_t, piece_t), (core, g_near, g_far, down_weight),
            in_specs=[smem()] + [vmem()] * 3, after=after,
        )

    hids = [hid_piece(0, part, ())]
    widths = (cut, units - cut)
    chips = call(
        functools.partial(add_cut_kernel, cut), "add_pre", tuple(jax.ShapeDtypeStruct((half, w), BF16) for w in widths),
        (keep_pre, other_pre), after=(hids[0][1],), cost=EARLY,
    )
    pre_parts = [[c] + [col_swap(c, k) for k in range(2, cols, 2)] for c in chips]
    hids.append(hid_piece(part, units - part, tuple(chips)))
    others = [col_swap(send, 1) for _, send in hids]
    chip_hid = call(add_kernel, "add_hid", bf_t, (*[k for k, _ in hids], *others))
    hid_parts = [chip_hid] + [col_swap(chip_hid, k) for k in range(2, cols, 2)]

    bias = up_bias.reshape(1, units)
    acts, slopes = zip(*[
        call(
            functools.partial(act_kernel, start), "act",
            (jax.ShapeDtypeStruct((half, w), BF16), jax.ShapeDtypeStruct((half, w), F32)), (*parts, bias),
            cost=EARLY,
        )
        for start, w, parts in zip((0, cut), widths, pre_parts)
    ])
    acts_far = [col_swap(a, 1) for a in acts]

    token_t = jax.ShapeDtypeStruct((8, 128), F32)
    down_t = jax.ShapeDtypeStruct((units, feats), F32)
    rt = divisor(cut, 256)
    down_half, wrote = call(
        functools.partial(down_kernel, 0, cut // rt, rt), "down_first", (down_t, token_t),
        (core, acts[0], acts_far[0], g_near, g_far), in_specs=[smem()] + [vmem()] * 4, out_specs=(anywhere(), vmem()),
        scratch=[pltpu.VMEM((SLOTS, rt, feats), F32), pltpu.SemaphoreType.DMA((SLOTS,))], after=(acts[1],),
    )
    pg = call(functools.partial(grad_kernel, cut), "pre_grad", bf_t, (*hid_parts, *slopes), after=(wrote, acts_far[1]))
    pg_far = col_swap(pg, 1)

    part_t = jax.ShapeDtypeStruct((half, feats), F32)
    rt = divisor(units - cut, 256)
    tiles = (units - cut) // rt
    down_grad, keep_in, send_in, bias_grad, pg_all = call(
        functools.partial(down_in_kernel, cut, tiles, rt), "down_last_in",
        (
            down_t, part_t, jax.ShapeDtypeStruct((half, feats), BF16), jax.ShapeDtypeStruct((1, units), F32),
            jax.ShapeDtypeStruct((2 * half, units), BF16),
        ),
        (core, pg, pg_far, up_weight, acts[1], acts_far[1], g_near, g_far, down_half),
        in_specs=[smem()] + [vmem()] * 7 + [anywhere()], out_specs=(anywhere(),) + (vmem(),) * 4, limit=24,
        scratch=[pltpu.VMEM((tiles, rt, feats), F32), pltpu.SemaphoreType.DMA((tiles,))], aliases={8: 0},
    )
    far_in = row_swap(send_in, 1)

    dt = divisor(feats, 128)
    dtiles = feats // dt
    first = max(1, dtiles * UP_FIRST // 12)
    up_t = jax.ShapeDtypeStruct((feats, units), F32)
    slots = [pltpu.VMEM((SLOTS, dt, units), F32), pltpu.SemaphoreType.DMA((SLOTS,))]
    up_half, wrote = call(
        functools.partial(up_kernel, 0, first, dt), "up_first", (up_t, token_t), (pg_all, x_near, x_far),
        in_specs=[vmem()] * 3, out_specs=(anywhere(), vmem()), scratch=slots, after=(send_in,),
    )
    share = call(sum_kernel, "share", part_t, (keep_in, far_in), after=(wrote,)).reshape(blocks, mine, feats)
    terms = [share[0]] + [row_swap(share[k // 2], k) for k in range(2, rows, 2)]
    up_grad, _ = call(
        functools.partial(up_kernel, first, dtiles, dt), "up_last", (up_t, token_t), (pg_all, x_near, x_far, up_half),
        in_specs=[vmem()] * 3 + [anywhere()], out_specs=(anywhere(), vmem()), scratch=slots, aliases={3: 0}, after=(share,),
    )
    in_grad = tree_sum(terms).astype(BF16)
    return (in_grad, up_grad, bias_grad.reshape(units), down_grad)


def solution(mesh):
    in_specs = (P("row", "col"), P("row", "col"), P("col", "row"), P("row"), P("row", "col"))
    out_specs = (P("row", "col"), P("col", "row"), P("row"), P("row", "col"))
    body = functools.partial(on_device, mesh.shape["row"], mesh.shape["col"])
    return jax.shard_map(body, mesh=mesh, in_specs=in_specs, out_specs=out_specs, check_vma=False)
```

```python
import functools
import math

import jax
import jax.numpy as jnp
from jax import lax
from jax.experimental import pallas as pl
from jax.experimental.pallas import tpu as pltpu
from jax.sharding import PartitionSpec as P

F32 = jnp.float32
BF16 = jnp.bfloat16
MIB = 1024 * 1024
SLOTS = 4
UP_FIRST = 4
EARLY = 16 * MIB
SCALE = 1000


def vmem():
    return pl.BlockSpec(memory_space=pltpu.VMEM)


def smem():
    return pl.BlockSpec(memory_space=pltpu.SMEM)


def anywhere():
    return pl.BlockSpec(memory_space=pl.ANY)


def call(kernel, name, out_shape, args, *, limit=16, in_specs=None, out_specs=None, scratch=(), aliases=None, after=(), cost=0):
    in_specs = in_specs if in_specs is not None else [vmem()] * len(args)
    body = kernel
    if after:
        n, m = len(args), len(args) + len(after)

        def body(*refs):
            kernel(*refs[:n], *refs[m:])

    return pl.pallas_call(
        body,
        out_shape=out_shape,
        in_specs=in_specs + [anywhere()] * len(after),
        out_specs=out_specs if out_specs is not None else jax.tree.map(lambda _: vmem(), out_shape),
        scratch_shapes=list(scratch),
        input_output_aliases=aliases or {},
        compiler_params=pltpu.CompilerParams(vmem_limit_bytes=limit * MIB),
        cost_estimate=pl.CostEstimate(flops=cost * SCALE, bytes_accessed=cost, transcendentals=0),
        name=name,
    )(*args, *after)


def tree_sum(terms):
    while len(terms) > 1:
        terms = [terms[i] + terms[i + 1] for i in range(0, len(terms), 2)]
    return terms[0]


def divisor(size, most):
    tile = min(size, most)
    while size % tile:
        tile -= 128
    return tile


def load_kernel(w_ref, o_ref, sem):
    copy = pltpu.make_async_copy(w_ref, o_ref, sem)
    copy.start()
    copy.wait()


def load(weight, name, limit, after):
    return call(
        load_kernel, name, pltpu.VMEM(weight.shape, weight.dtype), (weight,), limit=limit,
        in_specs=[anywhere()], out_specs=vmem(), scratch=[pltpu.SemaphoreType.DMA(())], after=after,
    )


def stack_kernel(a_ref, b_ref, o_ref, sems):
    copies = [pltpu.make_async_copy(r, o_ref.at[i], sems.at[i]) for i, r in enumerate((a_ref, b_ref))]
    for c in copies:
        c.start()
    for c in copies:
        c.wait()


def local_tokens(core, near_ref, far_ref):
    first = core == 0
    near, far = near_ref[...], far_ref[...]
    return jnp.concatenate([jnp.where(first, near, far), jnp.where(first, far, near)], axis=0)


def pre_kernel(core_ref, near_ref, far_ref, w_ref, keep_ref, send_ref):
    half, units = keep_ref.shape
    x = local_tokens(core_ref[0], near_ref, far_ref)
    tile = divisor(units, 512)
    for i in range(0, units, tile):
        out = jnp.dot(x, w_ref[:, i : i + tile], preferred_element_type=F32)
        keep_ref[:, i : i + tile] = out[:half]
        send_ref[:, i : i + tile] = out[half:]


def hid_kernel(start, core_ref, near_ref, far_ref, w_ref, keep_ref, send_ref):
    half, units = keep_ref.shape
    g = local_tokens(core_ref[0], near_ref, far_ref)
    tile = divisor(units, 512)
    for i in range(0, units, tile):
        w = w_ref[start + i : start + i + tile, :]
        out = lax.dot_general(w, g, (((1,), (1,)), ((), ())), preferred_element_type=F32).T
        keep_ref[:, i : i + tile] = out[:half]
        send_ref[:, i : i + tile] = out[half:]


def add_kernel(*refs):
    n, out_ref = len(refs) // 2, refs[-1]
    at = 0
    for a, b in zip(refs[:n], refs[n : 2 * n]):
        width = a.shape[1]
        out_ref[:, at : at + width] = (a[...] + b[...]).astype(BF16)
        at += width


def add_cut_kernel(cut, a_ref, b_ref, first_ref, second_ref):
    total = (a_ref[...] + b_ref[...]).astype(BF16)
    first_ref[...] = total[:, :cut]
    second_ref[...] = total[:, cut:]


def sum_kernel(a_ref, b_ref, out_ref):
    out_ref[...] = a_ref[...] + b_ref[...].astype(F32)


def act_kernel(start, *refs):
    parts, bias_ref, act_ref, slope_ref = refs[:-3], refs[-3], refs[-2], refs[-1]
    bias = bias_ref[:, start : start + act_ref.shape[1]].astype(F32)
    pre = tree_sum([r[...].astype(F32) for r in parts]) + bias
    cdf = 0.5 * (1.0 + lax.erf(pre * (1.0 / math.sqrt(2.0))))
    dens = jnp.exp(-0.5 * pre * pre) * (1.0 / math.sqrt(2.0 * math.pi))
    act_ref[...] = (pre * cdf).astype(BF16)
    slope_ref[...] = cdf + pre * dens


def grad_kernel(cut, *refs):
    parts, (slope_a, slope_b, out_ref) = refs[:-3], refs[-3:]
    hid = tree_sum([r[...].astype(F32) for r in parts])
    out_ref[:, :cut] = (hid[:, :cut] * slope_a[...]).astype(BF16)
    out_ref[:, cut:] = (hid[:, cut:] * slope_b[...]).astype(BF16)


def write_tiles(first, last, rows, make, out_ref, buf, sems):
    def copy(t):
        s = (t - first) % SLOTS
        return pltpu.make_async_copy(buf.at[s], out_ref.at[pl.ds(t * rows, rows), :], sems.at[s])

    for t in range(first, last):
        if t - first >= SLOTS:
            copy(t - SLOTS).wait()
        buf[(t - first) % SLOTS] = make(t * rows)
        copy(t).start()
    for t in range(max(first, last - SLOTS), last):
        copy(t).wait()


def outer(a, b):
    return lax.dot_general(a, b, (((0,), (0,)), ((), ())), preferred_element_type=F32)


def down_kernel(first, last, rows, core_ref, h0_ref, h1_ref, near_ref, far_ref, *refs):
    out_ref, done_ref, buf, sems = refs[-4:]
    done_ref[...] = jnp.zeros_like(done_ref)
    g = local_tokens(core_ref[0], near_ref, far_ref)

    def make(at):
        return outer(jnp.concatenate([h0_ref[:, at : at + rows], h1_ref[:, at : at + rows]], axis=0), g)

    write_tiles(first, last, rows, make, out_ref, buf, sems)


def down_in_kernel(
    base, last, rows, core_ref, p0_ref, p1_ref, w_ref, h0_ref, h1_ref, near_ref, far_ref, _, out_ref, keep_ref, send_ref, bias_ref, p_ref,
    buf, sems,
):
    near_first = core_ref[0] == 0
    g = local_tokens(core_ref[0], near_ref, far_ref)
    copies = [
        pltpu.make_async_copy(buf.at[t], out_ref.at[pl.ds(base + t * rows, rows), :], sems.at[t]) for t in range(last)
    ]
    for t in range(last):
        at = t * rows
        buf[t] = outer(jnp.concatenate([h0_ref[:, at : at + rows], h1_ref[:, at : at + rows]], axis=0), g)
        copies[t].start()
    half = p0_ref.shape[0]
    p0, p1 = p0_ref[...], p1_ref[...]
    p = jnp.concatenate([jnp.where(near_first, p0, p1), jnp.where(near_first, p1, p0)], axis=0)
    p_ref[...] = p
    feats = w_ref.shape[0]
    tile = divisor(feats, 512)
    for i in range(0, feats, tile):
        out = lax.dot_general(w_ref[i : i + tile, :], p, (((1,), (1,)), ((), ())), preferred_element_type=F32).T
        keep_ref[:, i : i + tile] = out[:half]
        send_ref[:, i : i + tile] = out[half:].astype(BF16)
    own = jnp.sum(p0.astype(F32), axis=0, keepdims=True)
    bias_ref[...] = own + jnp.sum(p1.astype(F32), axis=0, keepdims=True)
    for t in range(last):
        copies[t].wait()


def up_kernel(first, last, rows, p_ref, near_ref, far_ref, *refs):
    if first == 0:
        bias_ref, out_ref, done_ref, bias_out, buf, sems, bias_sem = refs
        done_ref[...] = jnp.zeros_like(done_ref)
        bias_copy = pltpu.make_async_copy(bias_ref, bias_out, bias_sem)
        bias_copy.start()
    else:
        _, out_ref, buf, sems = refs
    p = p_ref[...]

    def make(at):
        return outer(jnp.concatenate([near_ref[:, at : at + rows], far_ref[:, at : at + rows]], axis=0), p)

    write_tiles(first, last, rows, make, out_ref, buf, sems)
    if first == 0:
        bias_copy.wait()


def on_device(rows, cols, normed, out_grad, up_weight, up_bias, down_weight):
    mine, feats = normed.shape
    units = up_weight.shape[1]
    half = mine * rows // 2
    core = lax.rem(lax.axis_index("col"), 2).astype(jnp.int32).reshape(1)

    def row_swap(x, k):
        return lax.ppermute(x, "row", [(i, i ^ k) for i in range(rows)])

    def col_swap(x, k):
        return lax.ppermute(x, "col", [(i, i ^ k) for i in range(cols)])

    blocks = rows // 2
    stack = call(
        stack_kernel, "stack", pltpu.VMEM((2, mine, feats), BF16), (normed, out_grad),
        in_specs=[anywhere()] * 2, out_specs=vmem(), scratch=[pltpu.SemaphoreType.DMA((2,))], limit=58,
    )
    near = jnp.stack([stack] + [row_swap(stack, k) for k in range(2, rows, 2)], axis=1)
    near = near.reshape(2, half, feats)
    far = row_swap(near, 1)
    up_weight = load(up_weight, "load_up", 44, ())
    down_weight = load(down_weight, "load_down", 38, (near,))
    x_near, x_far, g_near, g_far = near[0], far[0], near[1], far[1]

    keep_t = jax.ShapeDtypeStruct((half, units), F32)
    bf_t = jax.ShapeDtypeStruct((half, units), BF16)
    keep_pre, send_pre = call(
        pre_kernel, "pre", (keep_t, keep_t), (core, x_near, x_far, up_weight), in_specs=[smem()] + [vmem()] * 3,
        after=(down_weight,),
    )
    other_pre = col_swap(send_pre, 1)

    part = units * 2 // 3 // 128 * 128
    cut = units // 2 // 128 * 128

    def hid_piece(start, width, after):
        piece_t = jax.ShapeDtypeStruct((half, width), F32)
        return call(
            functools.partial(hid_kernel, start), "hid", (piece_t, piece_t), (core, g_near, g_far, down_weight),
            in_specs=[smem()] + [vmem()] * 3, after=after,
        )

    hids = [hid_piece(0, part, ())]
    widths = (cut, units - cut)
    chips = call(
        functools.partial(add_cut_kernel, cut), "add_pre", tuple(jax.ShapeDtypeStruct((half, w), BF16) for w in widths),
        (keep_pre, other_pre), after=(hids[0][1],), cost=EARLY,
    )
    pre_parts = [[c] + [col_swap(c, k) for k in range(2, cols, 2)] for c in chips]
    hids.append(hid_piece(part, units - part, tuple(chips)))
    others = [col_swap(send, 1) for _, send in hids]
    chip_hid = call(add_kernel, "add_hid", bf_t, (*[k for k, _ in hids], *others))
    hid_parts = [chip_hid] + [col_swap(chip_hid, k) for k in range(2, cols, 2)]

    bias = up_bias.reshape(1, units)
    acts, slopes = zip(*[
        call(
            functools.partial(act_kernel, start), "act",
            (jax.ShapeDtypeStruct((half, w), BF16), jax.ShapeDtypeStruct((half, w), F32)), (*parts, bias),
            cost=EARLY,
        )
        for start, w, parts in zip((0, cut), widths, pre_parts)
    ])
    acts_far = [col_swap(a, 1) for a in acts]

    token_t = jax.ShapeDtypeStruct((8, 128), F32)
    down_t = jax.ShapeDtypeStruct((units, feats), F32)
    rt = divisor(cut, 256)
    down_half, wrote = call(
        functools.partial(down_kernel, 0, cut // rt, rt), "down_first", (down_t, token_t),
        (core, acts[0], acts_far[0], g_near, g_far), in_specs=[smem()] + [vmem()] * 4, out_specs=(anywhere(), vmem()),
        scratch=[pltpu.VMEM((SLOTS, rt, feats), F32), pltpu.SemaphoreType.DMA((SLOTS,))], after=(acts[1],),
    )
    pg = call(functools.partial(grad_kernel, cut), "pre_grad", bf_t, (*hid_parts, *slopes), after=(wrote, acts_far[1]))
    pg_far = col_swap(pg, 1)

    part_t = jax.ShapeDtypeStruct((half, feats), F32)
    rt = divisor(units - cut, 256)
    tiles = (units - cut) // rt
    down_grad, keep_in, send_in, bias_sum, pg_all = call(
        functools.partial(down_in_kernel, cut, tiles, rt), "down_last_in",
        (
            down_t, part_t, jax.ShapeDtypeStruct((half, feats), BF16), pltpu.VMEM((1, units), F32),
            jax.ShapeDtypeStruct((2 * half, units), BF16),
        ),
        (core, pg, pg_far, up_weight, acts[1], acts_far[1], g_near, g_far, down_half),
        in_specs=[smem()] + [vmem()] * 7 + [anywhere()], out_specs=(anywhere(),) + (vmem(),) * 4, limit=24,
        scratch=[pltpu.VMEM((tiles, rt, feats), F32), pltpu.SemaphoreType.DMA((tiles,))],
        aliases={8: 0},
    )
    far_in = row_swap(send_in, 1)

    dt = divisor(feats, 128)
    dtiles = feats // dt
    first = max(1, dtiles * UP_FIRST // 12)
    up_t = jax.ShapeDtypeStruct((feats, units), F32)
    slots = [pltpu.VMEM((SLOTS, dt, units), F32), pltpu.SemaphoreType.DMA((SLOTS,))]
    up_half, wrote, bias_grad = call(
        functools.partial(up_kernel, 0, first, dt), "up_first", (up_t, token_t, jax.ShapeDtypeStruct((1, units), F32)),
        (pg_all, x_near, x_far, bias_sum), in_specs=[vmem()] * 4, out_specs=(anywhere(), vmem(), anywhere()),
        scratch=slots + [pltpu.SemaphoreType.DMA(())], after=(send_in,),
    )
    share = call(sum_kernel, "share", part_t, (keep_in, far_in), after=(wrote,)).reshape(blocks, mine, feats)
    terms = [share[0]] + [row_swap(share[k // 2], k) for k in range(2, rows, 2)]
    up_grad = call(
        functools.partial(up_kernel, first, dtiles, dt), "up_last", up_t, (pg_all, x_near, x_far, up_half),
        in_specs=[vmem()] * 3 + [anywhere()], out_specs=anywhere(), scratch=slots, aliases={3: 0}, after=(share,),
    )
    in_grad = tree_sum(terms).astype(BF16)
    return (in_grad, up_grad, bias_grad.reshape(units), down_grad)


def solution(mesh):
    in_specs = (P("row", "col"), P("row", "col"), P("col", "row"), P("row"), P("row", "col"))
    out_specs = (P("row", "col"), P("col", "row"), P("row"), P("row", "col"))
    body = functools.partial(on_device, mesh.shape["row"], mesh.shape["col"])
    return jax.shard_map(body, mesh=mesh, in_specs=in_specs, out_specs=out_specs, check_vma=False)
```

```python
import functools
import math

import jax
import jax.numpy as jnp
from jax import lax
from jax.experimental import pallas as pl
from jax.experimental.pallas import tpu as pltpu
from jax.sharding import PartitionSpec as P

F32 = jnp.float32
BF16 = jnp.bfloat16
MIB = 1024 * 1024
SLOTS = 4
UP_FIRST = 4
EARLY = 16 * MIB
SCALE = 1000


def vmem():
    return pl.BlockSpec(memory_space=pltpu.VMEM)


def smem():
    return pl.BlockSpec(memory_space=pltpu.SMEM)


def anywhere():
    return pl.BlockSpec(memory_space=pl.ANY)


def call(kernel, name, out_shape, args, *, limit=16, in_specs=None, out_specs=None, scratch=(), aliases=None, after=(), cost=0):
    in_specs = in_specs if in_specs is not None else [vmem()] * len(args)
    body = kernel
    if after:
        n, m = len(args), len(args) + len(after)

        def body(*refs):
            kernel(*refs[:n], *refs[m:])

    return pl.pallas_call(
        body,
        out_shape=out_shape,
        in_specs=in_specs + [anywhere()] * len(after),
        out_specs=out_specs if out_specs is not None else jax.tree.map(lambda _: vmem(), out_shape),
        scratch_shapes=list(scratch),
        input_output_aliases=aliases or {},
        compiler_params=pltpu.CompilerParams(vmem_limit_bytes=limit * MIB),
        cost_estimate=pl.CostEstimate(flops=cost * SCALE, bytes_accessed=cost, transcendentals=0),
        name=name,
    )(*args, *after)


def tree_sum(terms):
    while len(terms) > 1:
        terms = [terms[i] + terms[i + 1] for i in range(0, len(terms), 2)]
    return terms[0]


def divisor(size, most):
    tile = min(size, most)
    while size % tile:
        tile -= 128
    return tile


def load_kernel(w_ref, o_ref, sem):
    copy = pltpu.make_async_copy(w_ref, o_ref, sem)
    copy.start()
    copy.wait()


def load(weight, name, limit, after):
    return call(
        load_kernel, name, pltpu.VMEM(weight.shape, weight.dtype), (weight,), limit=limit,
        in_specs=[anywhere()], out_specs=vmem(), scratch=[pltpu.SemaphoreType.DMA(())], after=after,
    )


def stack_kernel(a_ref, b_ref, o_ref, sems):
    copies = [pltpu.make_async_copy(r, o_ref.at[i], sems.at[i]) for i, r in enumerate((a_ref, b_ref))]
    for c in copies:
        c.start()
    for c in copies:
        c.wait()


def local_tokens(core, near_ref, far_ref):
    first = core == 0
    near, far = near_ref[...], far_ref[...]
    return jnp.concatenate([jnp.where(first, near, far), jnp.where(first, far, near)], axis=0)


def pre_kernel(core_ref, near_ref, far_ref, w_ref, keep_ref, send_ref):
    half, units = keep_ref.shape
    x = local_tokens(core_ref[0], near_ref, far_ref)
    tile = divisor(units, 512)
    for i in range(0, units, tile):
        out = jnp.dot(x, w_ref[:, i : i + tile], preferred_element_type=F32)
        keep_ref[:, i : i + tile] = out[:half]
        send_ref[:, i : i + tile] = out[half:]


def hid_kernel(start, core_ref, near_ref, far_ref, w_ref, keep_ref, send_ref):
    half, units = keep_ref.shape
    g = local_tokens(core_ref[0], near_ref, far_ref)
    tile = divisor(units, 512)
    for i in range(0, units, tile):
        w = w_ref[start + i : start + i + tile, :]
        out = lax.dot_general(w, g, (((1,), (1,)), ((), ())), preferred_element_type=F32).T
        keep_ref[:, i : i + tile] = out[:half]
        send_ref[:, i : i + tile] = out[half:]


def add_kernel(*refs):
    n, out_ref = len(refs) // 2, refs[-1]
    at = 0
    for a, b in zip(refs[:n], refs[n : 2 * n]):
        width = a.shape[1]
        out_ref[:, at : at + width] = (a[...] + b[...]).astype(BF16)
        at += width


def add_cut_kernel(cut, a_ref, b_ref, first_ref, second_ref):
    total = (a_ref[...] + b_ref[...]).astype(BF16)
    first_ref[...] = total[:, :cut]
    second_ref[...] = total[:, cut:]


def sum_kernel(a_ref, b_ref, out_ref):
    out_ref[...] = a_ref[...] + b_ref[...].astype(F32)


def act_kernel(start, *refs):
    parts, bias_ref, act_ref, slope_ref = refs[:-3], refs[-3], refs[-2], refs[-1]
    bias = bias_ref[:, start : start + act_ref.shape[1]].astype(F32)
    pre = tree_sum([r[...].astype(F32) for r in parts]) + bias
    cdf = 0.5 * (1.0 + lax.erf(pre * (1.0 / math.sqrt(2.0))))
    dens = jnp.exp(-0.5 * pre * pre) * (1.0 / math.sqrt(2.0 * math.pi))
    act_ref[...] = (pre * cdf).astype(BF16)
    slope_ref[...] = cdf + pre * dens


def grad_kernel(cut, *refs):
    parts, (slope_a, slope_b, out_ref) = refs[:-3], refs[-3:]
    hid = tree_sum([r[...].astype(F32) for r in parts])
    out_ref[:, :cut] = (hid[:, :cut] * slope_a[...]).astype(BF16)
    out_ref[:, cut:] = (hid[:, cut:] * slope_b[...]).astype(BF16)


def write_tiles(first, last, rows, make, out_ref, buf, sems):
    def copy(t):
        s = (t - first) % SLOTS
        return pltpu.make_async_copy(buf.at[s], out_ref.at[pl.ds(t * rows, rows), :], sems.at[s])

    width = out_ref.shape[1]
    cut = width // 4 // 128 * 128 or 128
    early = pltpu.make_async_copy(
        buf.at[0, :, pl.ds(0, cut)], out_ref.at[pl.ds(first * rows, rows), pl.ds(0, cut)], sems.at[SLOTS]
    )
    rest = pltpu.make_async_copy(
        buf.at[0, :, pl.ds(cut, width - cut)], out_ref.at[pl.ds(first * rows, rows), pl.ds(cut, width - cut)], sems.at[0]
    )
    buf[0, :, :cut] = make(first * rows, 0, cut)
    early.start()
    buf[0, :, cut:] = make(first * rows, cut, width)
    rest.start()

    def finish(t):
        if t == first:
            early.wait()
            rest.wait()
        else:
            copy(t).wait()

    for t in range(first + 1, last):
        if t - first >= SLOTS:
            finish(t - SLOTS)
        buf[(t - first) % SLOTS] = make(t * rows, 0, width)
        copy(t).start()
    for t in range(max(first, last - SLOTS), last):
        finish(t)


def outer(a, b):
    return lax.dot_general(a, b, (((0,), (0,)), ((), ())), preferred_element_type=F32)


def down_kernel(first, last, rows, core_ref, h0_ref, h1_ref, near_ref, far_ref, *refs):
    out_ref, done_ref, buf, sems = refs[-4:]
    done_ref[...] = jnp.zeros_like(done_ref)
    g = local_tokens(core_ref[0], near_ref, far_ref)

    def make(at, lo, hi):
        return outer(jnp.concatenate([h0_ref[:, at : at + rows], h1_ref[:, at : at + rows]], axis=0), g[:, lo:hi])

    write_tiles(first, last, rows, make, out_ref, buf, sems)


def down_in_kernel(
    base, last, rows, core_ref, p0_ref, p1_ref, w_ref, h0_ref, h1_ref, near_ref, far_ref, _, out_ref, keep_ref, send_ref, bias_ref, p_ref,
    buf, sems,
):
    near_first = core_ref[0] == 0
    g = local_tokens(core_ref[0], near_ref, far_ref)
    copies = [
        pltpu.make_async_copy(buf.at[t], out_ref.at[pl.ds(base + t * rows, rows), :], sems.at[t]) for t in range(last)
    ]
    for t in range(last):
        at = t * rows
        buf[t] = outer(jnp.concatenate([h0_ref[:, at : at + rows], h1_ref[:, at : at + rows]], axis=0), g)
        copies[t].start()
    half = p0_ref.shape[0]
    p0, p1 = p0_ref[...], p1_ref[...]
    p = jnp.concatenate([jnp.where(near_first, p0, p1), jnp.where(near_first, p1, p0)], axis=0)
    p_ref[...] = p
    feats = w_ref.shape[0]
    tile = divisor(feats, 512)
    for i in range(0, feats, tile):
        out = lax.dot_general(w_ref[i : i + tile, :], p, (((1,), (1,)), ((), ())), preferred_element_type=F32).T
        keep_ref[:, i : i + tile] = out[:half]
        send_ref[:, i : i + tile] = out[half:].astype(BF16)
    own = jnp.sum(p0.astype(F32), axis=0, keepdims=True)
    bias_ref[...] = own + jnp.sum(p1.astype(F32), axis=0, keepdims=True)
    for t in range(last):
        copies[t].wait()


def up_kernel(first, last, rows, p_ref, near_ref, far_ref, *refs):
    if first == 0:
        bias_ref, out_ref, done_ref, bias_out, buf, sems, bias_sem = refs
        done_ref[...] = jnp.zeros_like(done_ref)
        bias_copy = pltpu.make_async_copy(bias_ref, bias_out, bias_sem)
        bias_copy.start()
    else:
        _, out_ref, buf, sems = refs
    p = p_ref[...]

    def make(at, lo, hi):
        x = jnp.concatenate([near_ref[:, at : at + rows], far_ref[:, at : at + rows]], axis=0)
        return outer(x, p[:, lo:hi])

    write_tiles(first, last, rows, make, out_ref, buf, sems)
    if first == 0:
        bias_copy.wait()


def on_device(rows, cols, normed, out_grad, up_weight, up_bias, down_weight):
    mine, feats = normed.shape
    units = up_weight.shape[1]
    half = mine * rows // 2
    core = lax.rem(lax.axis_index("col"), 2).astype(jnp.int32).reshape(1)

    def row_swap(x, k):
        return lax.ppermute(x, "row", [(i, i ^ k) for i in range(rows)])

    def col_swap(x, k):
        return lax.ppermute(x, "col", [(i, i ^ k) for i in range(cols)])

    blocks = rows // 2
    stack = call(
        stack_kernel, "stack", pltpu.VMEM((2, mine, feats), BF16), (normed, out_grad),
        in_specs=[anywhere()] * 2, out_specs=vmem(), scratch=[pltpu.SemaphoreType.DMA((2,))], limit=58,
    )
    near = jnp.stack([stack] + [row_swap(stack, k) for k in range(2, rows, 2)], axis=1)
    near = near.reshape(2, half, feats)
    far = row_swap(near, 1)
    up_weight = load(up_weight, "load_up", 44, ())
    down_weight = load(down_weight, "load_down", 38, (near,))
    x_near, x_far, g_near, g_far = near[0], far[0], near[1], far[1]

    keep_t = jax.ShapeDtypeStruct((half, units), F32)
    bf_t = jax.ShapeDtypeStruct((half, units), BF16)
    keep_pre, send_pre = call(
        pre_kernel, "pre", (keep_t, keep_t), (core, x_near, x_far, up_weight), in_specs=[smem()] + [vmem()] * 3,
        after=(down_weight,),
    )
    other_pre = col_swap(send_pre, 1)

    part = units * 2 // 3 // 128 * 128
    cut = units // 2 // 128 * 128

    def hid_piece(start, width, after):
        piece_t = jax.ShapeDtypeStruct((half, width), F32)
        return call(
            functools.partial(hid_kernel, start), "hid", (piece_t, piece_t), (core, g_near, g_far, down_weight),
            in_specs=[smem()] + [vmem()] * 3, after=after,
        )

    hids = [hid_piece(0, part, ())]
    widths = (cut, units - cut)
    chips = call(
        functools.partial(add_cut_kernel, cut), "add_pre", tuple(jax.ShapeDtypeStruct((half, w), BF16) for w in widths),
        (keep_pre, other_pre), after=(hids[0][1],), cost=EARLY,
    )
    pre_parts = [[c] + [col_swap(c, k) for k in range(2, cols, 2)] for c in chips]
    hids.append(hid_piece(part, units - part, tuple(chips)))
    others = [col_swap(send, 1) for _, send in hids]
    chip_hid = call(add_kernel, "add_hid", bf_t, (*[k for k, _ in hids], *others))
    hid_parts = [chip_hid] + [col_swap(chip_hid, k) for k in range(2, cols, 2)]

    bias = up_bias.reshape(1, units)
    acts, slopes = zip(*[
        call(
            functools.partial(act_kernel, start), "act",
            (jax.ShapeDtypeStruct((half, w), BF16), jax.ShapeDtypeStruct((half, w), F32)), (*parts, bias),
            cost=EARLY,
        )
        for start, w, parts in zip((0, cut), widths, pre_parts)
    ])
    acts_far = [col_swap(a, 1) for a in acts]

    token_t = jax.ShapeDtypeStruct((8, 128), F32)
    down_t = jax.ShapeDtypeStruct((units, feats), F32)
    rt = divisor(cut, 256)
    down_half, wrote = call(
        functools.partial(down_kernel, 0, cut // rt, rt), "down_first", (down_t, token_t),
        (core, acts[0], acts_far[0], g_near, g_far), in_specs=[smem()] + [vmem()] * 4, out_specs=(anywhere(), vmem()),
        scratch=[pltpu.VMEM((SLOTS, rt, feats), F32), pltpu.SemaphoreType.DMA((SLOTS + 1,))], after=(acts[1],),
    )
    pg = call(functools.partial(grad_kernel, cut), "pre_grad", bf_t, (*hid_parts, *slopes), after=(wrote, acts_far[1]))
    pg_far = col_swap(pg, 1)

    part_t = jax.ShapeDtypeStruct((half, feats), F32)
    rt = divisor(units - cut, 256)
    tiles = (units - cut) // rt
    down_grad, keep_in, send_in, bias_sum, pg_all = call(
        functools.partial(down_in_kernel, cut, tiles, rt), "down_last_in",
        (
            down_t, part_t, jax.ShapeDtypeStruct((half, feats), BF16), pltpu.VMEM((1, units), F32),
            jax.ShapeDtypeStruct((2 * half, units), BF16),
        ),
        (core, pg, pg_far, up_weight, acts[1], acts_far[1], g_near, g_far, down_half),
        in_specs=[smem()] + [vmem()] * 7 + [anywhere()], out_specs=(anywhere(),) + (vmem(),) * 4, limit=24,
        scratch=[pltpu.VMEM((tiles, rt, feats), F32), pltpu.SemaphoreType.DMA((tiles,))],
        aliases={8: 0},
    )
    far_in = row_swap(send_in, 1)

    dt = divisor(feats, 128)
    dtiles = feats // dt
    first = max(1, dtiles * UP_FIRST // 12)
    up_t = jax.ShapeDtypeStruct((feats, units), F32)
    slots = [pltpu.VMEM((SLOTS, dt, units), F32), pltpu.SemaphoreType.DMA((SLOTS + 1,))]
    up_half, wrote, bias_grad = call(
        functools.partial(up_kernel, 0, first, dt), "up_first", (up_t, token_t, jax.ShapeDtypeStruct((1, units), F32)),
        (pg_all, x_near, x_far, bias_sum), in_specs=[vmem()] * 4, out_specs=(anywhere(), vmem(), anywhere()),
        scratch=slots + [pltpu.SemaphoreType.DMA(())], after=(send_in,),
    )
    share = call(sum_kernel, "share", part_t, (keep_in, far_in), after=(wrote,)).reshape(blocks, mine, feats)
    terms = [share[0]] + [row_swap(share[k // 2], k) for k in range(2, rows, 2)]
    up_grad = call(
        functools.partial(up_kernel, first, dtiles, dt), "up_last", up_t, (pg_all, x_near, x_far, up_half),
        in_specs=[vmem()] * 3 + [anywhere()], out_specs=anywhere(), scratch=slots, aliases={3: 0}, after=(share,),
    )
    in_grad = tree_sum(terms).astype(BF16)
    return (in_grad, up_grad, bias_grad.reshape(units), down_grad)


def solution(mesh):
    in_specs = (P("row", "col"), P("row", "col"), P("col", "row"), P("row"), P("row", "col"))
    out_specs = (P("row", "col"), P("col", "row"), P("row"), P("row", "col"))
    body = functools.partial(on_device, mesh.shape["row"], mesh.shape["col"])
    return jax.shard_map(body, mesh=mesh, in_specs=in_specs, out_specs=out_specs, check_vma=False)
```
